256 devices in a mesh: gx: 8 (over z_hi, core), gy: 4 (over y), gz: 8 (over x, z_lo).
Axes of the slice: x: 4, y: 4, z: 8 (z_hi: 4, z_lo: 2; z = z_hi * 2 + z_lo), core: 2. Of those that a mesh axis runs over, the one named last changes fastest.
Arguments:
- latent: bfloat16 [64, 64, 128, 256], P('gx', 'gy', 'gz'), may hold values from -700 to 700
- norm_gain: float32 [256], replicated, may hold values from 0.5 to 1.5
- norm_shift: float32 [256], replicated, may hold values from -3 to 3
- w_qkv: bfloat16 [256, 768], replicated, may hold values from -40 to 40
- w_out: bfloat16 [256, 256], replicated, may hold values from -0.375 to 0.375
- b_out: float32 [256], replicated, may hold values from -3 to 3
- depth_limit: int32 [16, 16, 32], P('gx', 'gy', 'gz'), may hold values from 0 to 1
Outputs:
- attended_out: bfloat16 [64, 64, 128, 256], P('gx', 'gy', 'gz')
The draws below stay inside these ranges and needn't reach their ends.
All inputs are finite; a program needn't handle non-finite values.
Results may differ from the reference program's by a relative error of at most 0.038.
Values may be sent and summed in bfloat16 or wider, within the bound.
No kernel may reach another device: no remote copies, remote signals or barrier semaphores. Data moves between devices by JAX's collectives and lax.ppermute only.
A program may use at most 128 MiB of HBM per device.

```python
import math
import jax
import jax.numpy as jnp
import numpy as np
from jax import lax

D = 256
HEADS = 8
GROUPS = 32
NX = 64
NY = 64
NZ = 128


def draw_latent(key, part):
    key = jax.random.fold_in(key, 1)
    first = jax.random.fold_in(key, 0)
    second = jax.random.fold_in(key, 1)
    fourth = jax.random.fold_in(key, 3)
    pos_x = jnp.arange(NX, dtype=jnp.float32) / NX
    pos_y = jnp.arange(NY, dtype=jnp.float32) / NY
    pos_z = jnp.arange(NZ, dtype=jnp.float32) / NZ
    rising = jnp.exp(math.log(3.0) * (pos_x[:, None, None] + pos_y[None, :, None] + pos_z[None, None, :]))[..., None] / 5.0
    cell_scale = jnp.exp(jax.random.uniform(second, (NX, NY, NZ, 1), jnp.float32) * math.log(10.0))
    common = jnp.clip(jax.random.normal(fourth, (D,), jnp.float32), -2.0, 2.0)
    base = jnp.clip(jax.random.normal(first, (NX, NY, NZ, D), jnp.float32), -6.0, 6.0) + common
    return (base * cell_scale * rising).astype(jnp.bfloat16)


def draw_w_qkv(key, part):
    key = jax.random.fold_in(key, 2)
    first = jax.random.fold_in(key, 0)
    base = jnp.clip(jax.random.normal(first, (D, 3 * D), jnp.float32), -6.0, 6.0) / math.sqrt(D)
    return base.astype(jnp.bfloat16)


def touch_ends(values, key, low, largest):
    shape = values.shape
    spot = [jax.random.randint(jax.random.fold_in(key, axis), (), 0, shape[axis]) for axis in range(len(shape))]
    values = values.at[tuple(spot)].set(low)
    longest = shape.index(max(shape))
    spot[longest] = (spot[longest] + 1) % shape[longest]
    return values.at[tuple(spot)].set(largest)


def gaussian(key, extent, scale, reach, held_as=jnp.bfloat16):
    values = jax.random.normal(key, extent, jnp.float32) * scale
    return jnp.minimum(jnp.maximum(values, -reach), reach).astype(held_as)


def setup_inputs(seed: int = 0) -> dict:
    arg_keys = jax.random.split(jax.random.key(seed), 8)
    latent = draw_latent(jax.random.fold_in(arg_keys[7], 71), 0)
    norm_gain = jnp.clip(1.0 + 0.1 * jax.random.normal(arg_keys[1], (D,), jnp.float32), 0.5, 1.5)
    norm_shift = gaussian(arg_keys[2], (D,), 0.5, 3.0, jnp.float32)
    w_qkv = draw_w_qkv(jax.random.fold_in(arg_keys[7], 71), 0)
    w_out = gaussian(arg_keys[4], (D, D), D ** -0.5, 0.375)
    b_out = gaussian(arg_keys[5], (D,), 0.5, 3.0, jnp.float32)
    depth_limit = touch_ends(jax.random.randint(arg_keys[6], (NX // 4, NY // 4, NZ // 4), 0, 2), jax.random.fold_in(arg_keys[6], 1), 0, 1).astype(jnp.int32)
    return {"latent": latent, "norm_gain": norm_gain, "norm_shift": norm_shift, "w_qkv": w_qkv, "w_out": w_out, "b_out": b_out, "depth_limit": depth_limit}


neighbour_offsets = [(first, second, third) for first in range(3) for second in range(3) for third in range(3)]

def to_blocks(field):
    size_x, size_y, size_z, chans = field.shape
    shaped = field.reshape(size_x // 4, 4, size_y // 4, 4, size_z // 4, 4, chans)
    return shaped.transpose(0, 2, 4, 1, 3, 5, 6).reshape(size_x // 4, size_y // 4, size_z // 4, 64, chans)

def from_blocks(blocks):
    count_x, count_y, count_z, cells, chans = blocks.shape
    shaped = blocks.reshape(count_x, count_y, count_z, 4, 4, 4, chans)
    return shaped.transpose(0, 3, 1, 4, 2, 5, 6).reshape(count_x * 4, count_y * 4, count_z * 4, chans)

def valid_table(limit, start_x, start_y, start_z, total_x, total_y, total_z):
    table = jnp.asarray(np.array(neighbour_offsets, dtype=np.int32) - 1)
    index_x = start_x + jnp.arange(limit.shape[0], dtype=jnp.int32)
    index_y = start_y + jnp.arange(limit.shape[1], dtype=jnp.int32)
    index_z = start_z + jnp.arange(limit.shape[2], dtype=jnp.int32)
    key_x = index_x[:, None] + table[None, :, 0]
    key_y = index_y[:, None] + table[None, :, 1]
    key_z = index_z[:, None] + table[None, :, 2]
    inside_x = (key_x >= 0) & (key_x < total_x)
    inside_y = (key_y >= 0) & (key_y < total_y)
    inside_z = (key_z >= 0) & (key_z < total_z)
    depth_ok = jnp.abs(table[:, 2])[None, None, None, :] <= limit[..., None]
    return inside_x[:, None, None, :] & inside_y[None, :, None, :] & inside_z[None, None, :, :] & depth_ok

def attend_span(query_blocks, region, valid, heads):
    depth = query_blocks.shape[1]
    width = query_blocks.shape[-1]
    head_dim = width // heads
    pieces = [region[first, second:second + 2, third:third + depth] for first, second, third in neighbour_offsets]
    keyvals = jnp.stack(pieces, axis=2).reshape(2, depth, 27 * 64, 2 * width)
    keys = keyvals[..., :width].reshape(2, depth, 27 * 64, heads, head_dim).astype(jnp.float32)
    values = keyvals[..., width:].reshape(2, depth, 27 * 64, heads, head_dim).astype(jnp.float32)
    queries = query_blocks.reshape(2, depth, 64, heads, head_dim).astype(jnp.float32)
    scores = jnp.einsum('abqhd,abkhd->abhqk', queries, keys) * head_dim ** (-0.5)
    allowed = jnp.repeat(valid, 64, axis=-1)
    scores = jnp.where(allowed[:, :, None, None, :], scores, jnp.float32(-1e+30))
    top = lax.optimization_barrier(jnp.max(scores, axis=-1, keepdims=True))
    expd = jnp.exp(scores - top)
    weights = (expd / lax.optimization_barrier(jnp.sum(expd, axis=-1, keepdims=True))).astype(jnp.bfloat16)
    mixed = jnp.einsum('abhqk,abkhd->abqhd', weights.astype(jnp.float32), values)
    return mixed.astype(jnp.bfloat16).reshape(2, depth, 64, width)

def attend_all(query_blocks, kv_blocks, valid, heads):
    count_x, count_y, count_z = query_blocks.shape[:3]
    width = query_blocks.shape[-1]
    pairs = count_y // 2
    zero = jnp.zeros((), jnp.int32)

    def one_span(index):
        block_x = (index // pairs).astype(jnp.int32)
        block_y = (index % pairs * 2).astype(jnp.int32)
        query_part = lax.dynamic_slice(query_blocks, (block_x, block_y, zero, zero, zero), (1, 2, count_z, 64, width))[0]
        region = lax.dynamic_slice(kv_blocks, (block_x, block_y, zero, zero, zero), (3, 4, count_z + 2, 64, 2 * width))
        valid_part = lax.dynamic_slice(valid, (block_x, block_y, zero, zero), (1, 2, count_z, 27))[0]
        return attend_span(query_part, region, valid_part, heads)
    result = lax.map(one_span, jnp.arange(count_x * pairs, dtype=jnp.int32))
    return result.reshape(count_x, count_y, count_z, 64, width)

def reference(latent, norm_gain, norm_shift, w_qkv, w_out, b_out, depth_limit):
    size_x, size_y, size_z, width = latent.shape
    grouped = latent.astype(jnp.float32).reshape(-1, GROUPS, width // GROUPS)
    count = grouped.shape[0] * grouped.shape[2]
    mean = lax.optimization_barrier(jnp.sum(grouped, axis=(0, 2))) / count
    centred = grouped - mean[None, :, None]
    var = lax.optimization_barrier(jnp.sum(centred * centred, axis=(0, 2))) / count
    normed = (centred * lax.rsqrt(var + 1e-06)[None, :, None]).reshape(size_x, size_y, size_z, width)
    normed = (normed * norm_gain + norm_shift).astype(jnp.bfloat16)
    qkv = jnp.dot(normed.reshape(-1, width), w_qkv, preferred_element_type=jnp.float32).astype(jnp.bfloat16)
    queries = qkv[:, :width].reshape(size_x, size_y, size_z, width)
    keyvals = qkv[:, width:].reshape(size_x, size_y, size_z, 2 * width)
    padded = jnp.pad(keyvals, ((4, 4), (4, 4), (4, 4), (0, 0)))
    valid = valid_table(depth_limit, 0, 0, 0, size_x // 4, size_y // 4, size_z // 4)
    mixed = from_blocks(attend_all(to_blocks(queries), to_blocks(padded), valid, HEADS))
    output = jnp.dot(mixed.reshape(-1, width), w_out, preferred_element_type=jnp.float32) + b_out
    return output.astype(jnp.bfloat16).reshape(size_x, size_y, size_z, width)
```

```python
import functools

import jax
import jax.numpy as jnp
import numpy as np
from jax import lax
from jax.experimental import pallas as pl
from jax.experimental.pallas import tpu as pltpu
from jax.sharding import PartitionSpec as P

HEADS = 8
GROUPS = 32
AXES = ("gx", "gy", "gz")
f32, bf = jnp.float32, jnp.bfloat16
NT = (((1,), (1,)), ((), ()))


def attn_kernel(
    scal, x_ref, mean_ref, mul_ref, shift_ref, wqT, wk, wvT, wo, bo, out_ref, n_ref, k_ref, vt_ref, qbd_ref, s_ref
):
    mean, mul, shift = mean_ref[...], mul_ref[...], shift_ref[...]

    def prep_col(c, carry):
        y, z = c // 6, c % 6
        ys, zs = scal[52 + y], scal[58 + z]
        xs = jnp.concatenate([x_ref[scal[48 + i], ys, zs] for i in range(4)], axis=0)
        n = ((xs.astype(f32) - mean) * mul + shift).astype(bf)
        n_ref[c] = n
        k_ref[c] = jnp.dot(n, wk[...], preferred_element_type=f32).astype(bf)
        vt = lax.dot_general(wvT[...], n, NT, preferred_element_type=f32)
        lane = lax.broadcasted_iota(jnp.int32, (1, 256), 1) // 64
        yz = scal[36 + y] * scal[42 + z]
        val = jnp.zeros((1, 256), f32)
        for i in range(4):
            val = jnp.where(lane == i, (scal[32 + i] * yz).astype(f32), val)
        vt = vt * val
        row = lax.broadcasted_iota(jnp.int32, (16, 256), 0)
        ones = jnp.where(row == 0, jnp.broadcast_to(val, (16, 256)), 0.0)
        for g in range(2):
            t = jnp.concatenate([vt[g * 128 : (g + 1) * 128], ones], axis=0)
            vt_ref[0, c, g] = t[:, :192].astype(bf)
            vt_ref[1, c, g] = pltpu.roll(t, 192, 1)[:, :192].astype(bf)
        return carry

    lax.fori_loop(0, 36, prep_col, 0)

    rr = lax.broadcasted_iota(jnp.int32, (128, 256), 0) // 32
    ll = lax.broadcasted_iota(jnp.int32, (128, 256), 1) // 64
    diag = rr == ll
    ri = lax.broadcasted_iota(jnp.int32, (64, 256), 0)
    li = lax.broadcasted_iota(jnp.int32, (64, 256), 1) % 64
    rT = jnp.where(ri == li, 1.0, 0.0).astype(bf)
    scale = float(np.log2(np.e) / np.sqrt(32.0))

    def query(i, carry):
        bx, by, bz = i // 16, (i // 4) % 4, i % 4
        c0 = (by + 1) * 6 + bz + 1
        nq = n_ref[c0, pl.ds(pl.multiple_of((bx + 1) * 64, 64), 64), :]
        n4 = jnp.concatenate([nq] * 4, axis=0)
        qt = lax.dot_general(wqT[...], n4, NT, preferred_element_type=f32)
        qt = (qt * scale).astype(bf)
        for g in range(2):
            qbd_ref[g] = jnp.where(diag, qt[g * 128 : (g + 1) * 128], jnp.zeros((), bf))
        r0 = pl.multiple_of(bx * 64, 64)

        def body(cols):
            tops = []
            for g in range(2):
                m = None
                for j, (dy, dz) in enumerate(cols):
                    c = (by + dy) * 6 + bz + dz
                    kt = k_ref[c, pl.ds(r0, 192), g * 128 : (g + 1) * 128]
                    s = jnp.dot(kt, qbd_ref[g], preferred_element_type=f32)
                    s_ref[g, j] = s
                    mm = jnp.max(s.reshape(24, 8, 256), axis=0)
                    m = mm if m is None else jnp.maximum(m, mm)
                tops.append(jnp.max(m, axis=0, keepdims=True))
            mixed = []
            for g in range(2):
                o = jnp.zeros((144, 256), f32)
                for j, (dy, dz) in enumerate(cols):
                    c = (by + dy) * 6 + bz + dz
                    p = jnp.exp2(s_ref[g, j] - tops[g]).astype(bf)
                    o = o + jnp.dot(vt_ref[bx, c, g], p, preferred_element_type=f32)
                om = o[:128] * (1.0 / o[128:129])
                om = jnp.where(diag, om, 0.0).astype(bf)
                mixed.append(lax.dot_general(rT, om, NT, preferred_element_type=f32).astype(bf))
            out = jnp.dot(jnp.concatenate(mixed, axis=1), wo[...], preferred_element_type=f32) + bo[...]
            out_ref[bx, by, bz] = out.astype(bf)

        limit = scal[i]

        @pl.when(limit == 0)
        def _near():
            body([(dy, 1) for dy in range(3)])

        @pl.when(limit != 0)
        def _full():
            body([(dy, dz) for dz in range(3) for dy in range(3)])

        return carry

    lax.fori_loop(0, 32, query, 0)


def attend(*args):
    vmem = pl.BlockSpec(memory_space=pltpu.VMEM)
    return pl.pallas_call(
        attn_kernel,
        out_shape=jax.ShapeDtypeStruct((2, 4, 4, 64, 256), bf),
        in_specs=[pl.BlockSpec(memory_space=pltpu.SMEM)] + [vmem] * 9,
        out_specs=vmem,
        scratch_shapes=[
            pltpu.VMEM((36, 256, 256), bf),
            pltpu.VMEM((36, 256, 256), bf),
            pltpu.VMEM((2, 36, 2, 144, 192), bf),
            pltpu.VMEM((2, 128, 256), bf),
            pltpu.VMEM((2, 9, 192, 256), f32),
        ],
        compiler_params=pltpu.CompilerParams(vmem_limit_bytes=56 * 2**20),
    )(*args)


def to_blocks(field):
    size_x, size_y, size_z, chans = field.shape
    shaped = field.reshape(size_x // 4, 4, size_y // 4, 4, size_z // 4, 4, chans)
    return shaped.transpose(0, 2, 4, 1, 3, 5, 6).reshape(size_x // 4, size_y // 4, size_z // 4, 64, chans)


def from_blocks(blocks):
    count_x, count_y, count_z, cells, chans = blocks.shape
    shaped = blocks.reshape(count_x, count_y, count_z, 4, 4, 4, chans)
    return shaped.transpose(0, 3, 1, 4, 2, 5, 6).reshape(count_x * 4, count_y * 4, count_z * 4, chans)


def padded(blocks, axis, dim):
    count = lax.axis_size(axis)
    head = lax.slice_in_dim(blocks, 0, 1, axis=dim)
    tail = lax.slice_in_dim(blocks, blocks.shape[dim] - 1, blocks.shape[dim], axis=dim)
    up = [(i, i + 1) for i in range(count - 1)]
    down = [(i + 1, i) for i in range(count - 1)]
    return jnp.concatenate(
        [lax.ppermute(tail, axis, up), blocks, lax.ppermute(head, axis, down)], axis=dim
    )


def group_stats(latent):
    width = latent.shape[-1]
    cells = latent.astype(f32).reshape(-1, width)
    per = width // GROUPS
    entries = cells.shape[0] * per
    means = jnp.sum(jnp.sum(cells, axis=0).reshape(GROUPS, per), axis=1) / entries
    centred = cells - jnp.repeat(means, per)[None, :]
    squares = jnp.sum(jnp.sum(centred * centred, axis=0).reshape(GROUPS, per), axis=1)
    count = lax.axis_size(AXES)
    mine = jnp.concatenate([means, squares, jnp.zeros((64,), f32)])
    every = lax.all_to_all(jnp.broadcast_to(mine[None], (count, 128)), AXES, 0, 0, tiled=True)
    mean = jnp.sum(every[:, :32], axis=0) / count
    apart = every[:, :32] - mean[None]
    var = (jnp.sum(every[:, 32:64], axis=0) / entries + jnp.sum(apart * apart, axis=0)) / count
    return mean, var


def scalars(depth_limit):
    parts, sources = [depth_limit.reshape(-1)], []
    for axis, inner in zip(AXES, depth_limit.shape):
        spots = np.arange(inner + 2)
        index, ends = lax.axis_index(axis), lax.axis_size(axis) - 1
        outside = ((spots == 0) & (index == 0)) | ((spots == inner + 1) & (index == ends))
        parts.append(1 - outside.astype(jnp.int32))
        sources.append(jnp.where(outside, np.clip(spots, 1, inner), spots).astype(jnp.int32))
    return jnp.concatenate(parts + sources)


def on_device(latent, norm_gain, norm_shift, w_qkv, w_out, b_out, depth_limit):
    width = latent.shape[-1]
    blocks = to_blocks(latent)
    for axis, dim in (("gz", 2), ("gx", 0), ("gy", 1)):
        blocks = padded(blocks, axis, dim)
    mean, var = group_stats(latent)
    per = width // GROUPS
    mul = jnp.repeat(lax.rsqrt(var + 1e-06), per) * norm_gain
    mean = jnp.repeat(mean, per)
    out = attend(
        scalars(depth_limit),
        blocks,
        mean[None],
        mul[None],
        norm_shift[None],
        w_qkv[:, :width].T,
        w_qkv[:, width : 2 * width],
        w_qkv[:, 2 * width :].T,
        w_out,
        b_out[None],
    )
    return from_blocks(out)


def solution(mesh):
    placed = (P("gx", "gy", "gz", None), P(), P(), P(), P(), P(), P("gx", "gy", "gz"))
    return jax.shard_map(
        on_device, mesh=mesh, in_specs=placed, out_specs=P("gx", "gy", "gz", None), check_vma=False
    )
```

```python
import functools

import jax
import jax.numpy as jnp
import numpy as np
from jax import lax
from jax.experimental import pallas as pl
from jax.experimental.pallas import tpu as pltpu
from jax.sharding import PartitionSpec as P

GROUPS = 32
AXES = ("gx", "gy", "gz")
f32, bf = jnp.float32, jnp.bfloat16
NT = (((1,), (1,)), ((), ()))
SCALE = float(np.log2(np.e) / np.sqrt(32.0))
VMEM = pl.BlockSpec(memory_space=pltpu.VMEM)
SMEM = pl.BlockSpec(memory_space=pltpu.SMEM)
HBM = pl.BlockSpec(memory_space=pl.ANY)


def iota(shape, dim):
    return lax.broadcasted_iota(jnp.int32, shape, dim)


def exact_dot(a, b):
    return jnp.dot(a, b, precision=lax.Precision.HIGHEST, preferred_element_type=f32)


def low_rows(a, b):
    return jnp.where(iota(a.shape, 0) < 4, a, pltpu.roll(b, 4, 0))


def high_rows(a, b):
    return jnp.where(iota(a.shape, 0) < 4, pltpu.roll(a, 4, 0), b)


def arrange_kernel(x_ref, own_ref, low_ref, high_ref):
    for bx in range(2):
        for by in range(4):

            def plane(x, carry, bx=bx, by=by):
                for half in range(2):
                    lows, highs = [], []
                    for pair in range(2):
                        a, b = [
                            x_ref[bx * 4 + x, by * 4 + pair * 2 + k, half * 8 : half * 8 + 8].astype(f32)
                            for k in range(2)
                        ]
                        lows.append(low_rows(a, b))
                        highs.append(high_rows(a, b))
                    rows = pl.ds(pl.multiple_of(x * 16, 16), 16)
                    for k, parts in enumerate((lows, highs)):
                        piece = jnp.concatenate(parts, axis=0).astype(bf)
                        own_ref[bx, by, half * 2 + k, rows] = piece
                        if (half, k) == (0, 0):
                            low_ref[bx, by, rows] = piece
                        if (half, k) == (1, 1):
                            high_ref[bx, by, rows] = piece
                return carry

            lax.fori_loop(0, 4, plane, 0, unroll=True)


def arrange(latent):
    return pl.pallas_call(
        arrange_kernel,
        out_shape=[
            jax.ShapeDtypeStruct((2, 4, 4, 64, 256), bf),
            jax.ShapeDtypeStruct((2, 4, 64, 256), bf),
            jax.ShapeDtypeStruct((2, 4, 64, 256), bf),
        ],
        in_specs=[VMEM],
        out_specs=[VMEM] * 3,
        compiler_params=pltpu.CompilerParams(vmem_limit_bytes=24 * 2**20),
    )(latent)


def stats_kernel(x_ref, after_a, after_b, row_ref):
    entries = 2048 * 8

    def sums(i, acc):
        return acc + jnp.sum(x_ref[i].astype(f32).reshape(32, 8, 256), axis=0)

    zeros = jnp.zeros((8, 256), f32)
    total = lax.fori_loop(0, 8, sums, zeros)
    total = jnp.broadcast_to(jnp.sum(total, axis=0, keepdims=True), (8, 256)) * (1.0 / entries)
    same = (iota((256, 256), 0) // 8 == iota((256, 256), 1) // 8).astype(f32)
    mean = exact_dot(total, same)

    def squares(i, acc):
        cells = x_ref[i].astype(f32) - mean[:1][None]
        return acc + jnp.sum((cells * cells).reshape(32, 8, 256), axis=0)

    acc = lax.fori_loop(0, 8, squares, zeros)
    acc = jnp.broadcast_to(jnp.sum(acc, axis=0, keepdims=True), (8, 256))
    first = (iota((256, 128), 0) // 8 == iota((256, 128), 1)).astype(f32)
    second = (iota((256, 128), 0) // 8 + 32 == iota((256, 128), 1)).astype(f32)
    row = exact_dot(total, first) + exact_dot(acc, second)
    row_ref[...] = jnp.broadcast_to(row[:1], row_ref.shape)


def stats(latent, *after):
    return pl.pallas_call(
        stats_kernel,
        out_shape=jax.ShapeDtypeStruct((256, 128), f32),
        in_specs=[VMEM] + [HBM] * 2,
        out_specs=VMEM,
        compiler_params=pltpu.CompilerParams(vmem_limit_bytes=16 * 2**20),
    )(latent, *after)


def interleave(*stages):
    stages = list(stages)
    while stages:
        for stage in list(stages):
            if next(stage, True):
                stages.remove(stage)


def attend_kernel(ends, edge, limit, *refs):
    if edge:
        own, zlow, zhigh, xlow, xhigh, ylow, yhigh, done, *refs = refs
    else:
        own, zlow, zhigh, xlow, xhigh, *refs = refs
    every, gain, shift_ref, w_qkv, wqT, wvT, wo, bo, out_ref, *refs = refs
    x_ref, k_ref, vt_ref, qbd_ref, om_ref, s_ref, p_ref, m_ref, lists, sems, wk = refs
    copies = [
        (own, x_ref.at[1:3, 1:5, 1:5]),
        (zlow, x_ref.at[1:3, 1:5, 0]),
        (zhigh, x_ref.at[1:3, 1:5, 5]),
        (xlow, x_ref.at[0, 1:5]),
        (xhigh, x_ref.at[3, 1:5]),
    ]
    if edge:
        copies += [(ylow, x_ref.at[:, 0]), (yhigh, x_ref.at[:, 5]), (done, out_ref.at[:, 4:12])]
    copies = [pltpu.make_async_copy(a, b, sems.at[i]) for i, (a, b) in enumerate(copies)]
    for copy in copies:
        copy.start()

    spots = [lax.axis_index(axis) for axis in AXES]
    first = [(spot == 0).astype(jnp.int32) for spot in spots]
    last = [(spot == end).astype(jnp.int32) for spot, end in zip(spots, ends)]

    def place(dim, inner, i):
        out = jnp.where(i == 0, first[dim], jnp.where(i == inner + 1, last[dim], 0))
        return 1 - out, jnp.where(out == 0, i, jnp.where(i == 0, 1, inner))

    wk[...] = w_qkv[:, 256:512]
    entries = 2048.0 * 8.0
    rows = every[...]
    means = jnp.sum(rows, axis=0, keepdims=True) * (1.0 / 256)
    apart = rows - means
    spread = jnp.sum(apart * apart, axis=0, keepdims=True)
    first_of = (iota((128, 256), 0) == iota((128, 256), 1) // 8).astype(f32)
    second_of = (iota((128, 256), 0) == iota((128, 256), 1) // 8 + 32).astype(f32)
    means8, spread8 = jnp.broadcast_to(means, (8, 128)), jnp.broadcast_to(spread, (8, 128))
    mean = exact_dot(means8, first_of)[:1]
    var = (exact_dot(means8, second_of)[:1] * 256 / entries + exact_dot(spread8, first_of)[:1]) * (1.0 / 256)
    mul = lax.rsqrt(var + 1e-06) * gain[...]
    shift = shift_ref[...]

    bys = (0, 3) if edge else (1, 2)

    def sort(i, counts):
        deep, flat = counts
        bx, k, bz = i // 8, (i // 4) % 2, i % 4
        by = k * 3 if edge else k + 1
        spot = bx * 16 + by * 4 + bz
        lists[0, deep] = spot
        lists[1, flat] = spot
        is_deep = (limit[bx, by, bz] != 0).astype(jnp.int32)
        return deep + is_deep, flat + 1 - is_deep

    zero = jnp.int32(0)
    deep, flat = lax.fori_loop(0, 16, sort, (zero, zero))

    own_head = iota((256, 512), 0) // 32 == iota((256, 512), 1) // 64
    diag = iota((128, 256), 0) // 32 == iota((128, 256), 1) // 64
    for copy in copies[:7]:
        copy.wait()

    def normed(cells):
        return ((cells.astype(f32) - mean) * mul + shift).astype(bf)

    lane = iota((1, 256), 1) // 64
    marks = jnp.zeros((1, 256), f32)
    for i in range(4):
        marks = jnp.where(lane == i, place(0, 2, i)[0].astype(f32), marks)
    tick = iota((16, 256), 0) == 0

    def prep_column(c, carry):
        if not edge:
            c = c + 6
        y, z = c // 6, c % 6
        (y_in, y_from), (z_in, z_from) = place(1, 4, y), place(2, 4, z)
        n = normed(
            jnp.concatenate([x_ref[place(0, 2, i)[1], y_from, z_from] for i in range(4)], axis=0)
        )
        k_ref[c] = jnp.dot(n, wk[...], preferred_element_type=f32).astype(bf)
        valid = marks * (y_in * z_in).astype(f32)
        vt = lax.dot_general(wvT[...], n, NT, preferred_element_type=f32) * valid
        ones = jnp.where(tick, jnp.broadcast_to(valid, (16, 256)), 0.0)
        for g in range(2):
            t = jnp.concatenate([vt[g * 128 : (g + 1) * 128], ones], axis=0)
            vt_ref[0, c, g] = t[:, :192].astype(bf)
            vt_ref[1, c, g] = pltpu.roll(t, 192, 1)[:, :192].astype(bf)
        return carry

    lax.fori_loop(0, 36 if edge else 24, prep_column, 0, unroll=4)

    def prep_query(i, carry):
        bx, k, bz = i // 8, (i // 4) % 2, i % 4
        by = k * 3 if edge else k + 1
        n = normed(x_ref[bx + 1, by + 1, bz + 1])
        q = lax.dot_general(wqT[...], jnp.concatenate([n] * 4, axis=0), NT, preferred_element_type=f32) * SCALE
        qbd_ref[bx * 16 + by * 4 + bz] = jnp.where(own_head, jnp.concatenate([q, q], axis=1), 0.0).astype(bf)
        return carry

    lax.fori_loop(0, 16, prep_query, 0, unroll=4)

    def columns(i, cols):
        by, bz = (i // 4) % 4, i % 4
        return [(by + dy) * 6 + bz + dz for dy, dz in cols]

    def scores(i, cols):
        rows = pl.ds(pl.multiple_of(i // 16 * 64, 64), 192)
        q, m, spots = qbd_ref[i], None, columns(i, cols)
        for j in range(0, len(cols), 3):
            keys = jnp.concatenate([k_ref[c, rows] for c in spots[j : j + 3]], axis=0)
            s = jnp.dot(keys, q, preferred_element_type=f32)
            s_ref[j * 192 : (j + 3) * 192] = s
            top = jnp.max(s.reshape(-1, 8, 512), axis=0)
            m = top if m is None else jnp.maximum(m, top)
            yield False
        m_ref[...] = jnp.broadcast_to(jnp.max(m, axis=0, keepdims=True), (8, 512))

    def weights(cols):
        top = m_ref[...][:1]
        for j in range(0, len(cols), 3):
            part = slice(j * 192, (j + 3) * 192)
            p_ref[part] = jnp.exp2(s_ref[part] - top).astype(bf)
            yield False

    def mix(i, cols):
        o = [None, None]
        for j, c in enumerate(columns(i, cols)):
            for g in range(2):
                part = jnp.dot(
                    vt_ref[i // 16, c, g],
                    p_ref[j * 192 : (j + 1) * 192, g * 256 : (g + 1) * 256],
                    preferred_element_type=f32,
                )
                o[g] = part if o[g] is None else o[g] + part
            if j % 3 == 2:
                yield False
        for g in range(2):
            om_ref[i, g] = jnp.where(diag, o[g][:128] * (1.0 / o[g][128:129]), 0.0).astype(bf)

    def run(which, count, cols):
        def step(t, carry):
            now = lists[which, jnp.minimum(t, count - 1)]
            before = lists[which, jnp.maximum(t - 1, 0)]
            interleave(weights(cols), scores(now, cols), mix(before, cols))
            return carry

        lax.fori_loop(0, jnp.where(count > 0, count + 1, 0), step, 0)

    run(0, deep, [(dy, dz) for dz in range(3) for dy in range(3)])
    run(1, flat, [(dy, 1) for dy in range(3)])

    pick = jnp.where(iota((64, 256), 0) == iota((64, 256), 1) % 64, 1.0, 0.0).astype(bf)
    if edge:
        copies[7].wait()

    def finish(i, carry):
        bx, k = i // 2, i % 2
        by = k * 3 if edge else k + 1
        spot = bx * 16 + by * 4
        mixed = [
            jnp.concatenate(
                [lax.dot_general(pick, om_ref[spot + bz, g], NT, preferred_element_type=f32).astype(bf) for g in range(2)],
                axis=1,
            )
            for bz in range(4)
        ]
        out = jnp.dot(jnp.concatenate(mixed, axis=0), wo[...], preferred_element_type=f32) + bo[...]
        y0 = by * 4 if edge else k * 4
        for x in range(4):
            for pair in range(2):
                parts = [out[b * 64 + x * 16 + pair * 8 : b * 64 + x * 16 + pair * 8 + 8] for b in range(4)]
                for which, join in enumerate((low_rows, high_rows)):
                    line = jnp.concatenate([join(parts[0], parts[1]), join(parts[2], parts[3])], axis=0)
                    out_ref[bx * 4 + x, y0 + pair * 2 + which] = line.astype(bf)
        return carry

    lax.fori_loop(0, 4, finish, 0, unroll=2)


def attend(ends, edge, limit, halos, *consts):
    out_y = 16 if edge else 8
    return pl.pallas_call(
        functools.partial(attend_kernel, ends, edge),
        out_shape=jax.ShapeDtypeStruct((8, out_y, 16, 256), bf),
        in_specs=[SMEM] + [HBM] * len(halos) + [VMEM] * len(consts),
        out_specs=VMEM,
        scratch_shapes=[
            pltpu.VMEM((4, 6, 6, 64, 256), bf),
            pltpu.VMEM((36, 256, 256), bf),
            pltpu.VMEM((2, 36, 2, 144, 192), bf),
            pltpu.VMEM((32, 256, 512), bf),
            pltpu.VMEM((32, 2, 128, 256), bf),
            pltpu.VMEM((1728, 512), f32),
            pltpu.VMEM((1728, 512), bf),
            pltpu.VMEM((8, 512), f32),
            pltpu.SMEM((2, 17), jnp.int32),
            pltpu.SemaphoreType.DMA((8,)),
            pltpu.VMEM((256, 256), bf),
        ],
        compiler_params=pltpu.CompilerParams(vmem_limit_bytes=50 * 2**20),
        cost_estimate=pl.CostEstimate(flops=15 * 10**9, bytes_accessed=8 * 10**6, transcendentals=14 * 10**6),
    )(limit, *halos, *consts)


def swap(low, high, axis):
    count = lax.axis_size(axis)
    up = [(i, i + 1) for i in range(count - 1)]
    down = [(i + 1, i) for i in range(count - 1)]
    return lax.ppermute(high, axis, up), lax.ppermute(low, axis, down)


def on_device(latent, norm_gain, norm_shift, w_qkv, w_out, b_out, depth_limit):
    width = latent.shape[-1]
    own, face_low, face_high = arrange(latent)
    zlow, zhigh = swap(face_low, face_high, "gz")

    def deep_layer(x):
        return jnp.concatenate([zlow[x, :, None], own[x], zhigh[x, :, None]], axis=1)

    xsend = deep_layer(0), deep_layer(1)
    xlow, xhigh = swap(*xsend, "gx")
    every = lax.all_to_all(stats(latent, *xsend), AXES, 0, 0, tiled=True)

    def deep_row(y):
        inner = jnp.concatenate([zlow[:, y, None], own[:, y], zhigh[:, y, None]], axis=1)
        return jnp.concatenate([xlow[y][None], inner, xhigh[y][None]], axis=0)

    ylow, yhigh = swap(deep_row(0), deep_row(3), "gy")
    consts = (
        every,
        norm_gain[None],
        norm_shift[None],
        w_qkv,
        w_qkv[:, :width].T,
        w_qkv[:, 2 * width :].T,
        w_out,
        b_out[None],
    )
    ends = tuple(lax.axis_size(axis) - 1 for axis in AXES)
    halos = (own, zlow, zhigh, xlow, xhigh)
    middle = attend(ends, False, depth_limit, halos, *consts)
    return attend(ends, True, depth_limit, halos + (ylow, yhigh, middle), *consts)


def solution(mesh):
    placed = (P("gx", "gy", "gz", None), P(), P(), P(), P(), P(), P("gx", "gy", "gz"))
    return jax.shard_map(
        on_device, mesh=mesh, in_specs=placed, out_specs=P("gx", "gy", "gz", None), check_vma=False
    )
```

```python
import functools

import jax
import jax.numpy as jnp
import numpy as np
from jax import lax
from jax.experimental import pallas as pl
from jax.experimental.pallas import tpu as pltpu
from jax.sharding import PartitionSpec as P

GROUPS = 32
AXES = ("gx", "gy", "gz")
f32, bf = jnp.float32, jnp.bfloat16
NT = (((1,), (1,)), ((), ()))
SCALE = float(np.log2(np.e) / np.sqrt(32.0))
VMEM = pl.BlockSpec(memory_space=pltpu.VMEM)
SMEM = pl.BlockSpec(memory_space=pltpu.SMEM)
HBM = pl.BlockSpec(memory_space=pl.ANY)


def iota(shape, dim):
    return lax.broadcasted_iota(jnp.int32, shape, dim)


def exact_dot(a, b):
    return jnp.dot(a, b, precision=lax.Precision.HIGHEST, preferred_element_type=f32)


def low_rows(a, b):
    return jnp.where(iota(a.shape, 0) < 4, a, pltpu.roll(b, 4, 0))


def high_rows(a, b):
    return jnp.where(iota(a.shape, 0) < 4, pltpu.roll(a, 4, 0), b)


def arrange_kernel(x_ref, own_ref, low_ref, high_ref):
    for bx in range(2):
        for by in range(4):

            def plane(x, carry, bx=bx, by=by):
                for half in range(2):
                    lows, highs = [], []
                    for pair in range(2):
                        a, b = [
                            x_ref[bx * 4 + x, by * 4 + pair * 2 + k, half * 8 : half * 8 + 8].astype(f32)
                            for k in range(2)
                        ]
                        lows.append(low_rows(a, b))
                        highs.append(high_rows(a, b))
                    rows = pl.ds(pl.multiple_of(x * 16, 16), 16)
                    for k, parts in enumerate((lows, highs)):
                        piece = jnp.concatenate(parts, axis=0).astype(bf)
                        own_ref[bx, by, half * 2 + k, rows] = piece
                        if (half, k) == (0, 0):
                            low_ref[bx, by, rows] = piece
                        if (half, k) == (1, 1):
                            high_ref[bx, by, rows] = piece
                return carry

            lax.fori_loop(0, 4, plane, 0, unroll=True)


def arrange(latent):
    return pl.pallas_call(
        arrange_kernel,
        out_shape=[
            jax.ShapeDtypeStruct((2, 4, 4, 64, 256), bf),
            jax.ShapeDtypeStruct((2, 4, 64, 256), bf),
            jax.ShapeDtypeStruct((2, 4, 64, 256), bf),
        ],
        in_specs=[VMEM],
        out_specs=[VMEM] * 3,
        compiler_params=pltpu.CompilerParams(vmem_limit_bytes=24 * 2**20),
    )(latent)


def stats_kernel(x_ref, w_ref, row_ref, wqT_ref, wvT_ref):
    wqT_ref[...] = w_ref[:, :256].astype(f32).T.astype(bf)
    wvT_ref[...] = w_ref[:, 512:].astype(f32).T.astype(bf)
    entries = 2048 * 8

    def sums(i, acc):
        return acc + jnp.sum(x_ref[i].astype(f32).reshape(32, 8, 256), axis=0)

    zeros = jnp.zeros((8, 256), f32)
    total = lax.fori_loop(0, 8, sums, zeros)
    total = jnp.broadcast_to(jnp.sum(total, axis=0, keepdims=True), (8, 256)) * (1.0 / entries)
    same = (iota((256, 256), 0) // 8 == iota((256, 256), 1) // 8).astype(f32)
    mean = exact_dot(total, same)

    def squares(i, acc):
        cells = x_ref[i].astype(f32) - mean[:1][None]
        return acc + jnp.sum((cells * cells).reshape(32, 8, 256), axis=0)

    acc = lax.fori_loop(0, 8, squares, zeros)
    acc = jnp.broadcast_to(jnp.sum(acc, axis=0, keepdims=True), (8, 256))
    first = (iota((256, 128), 0) // 8 == iota((256, 128), 1)).astype(f32)
    second = (iota((256, 128), 0) // 8 + 32 == iota((256, 128), 1)).astype(f32)
    row = exact_dot(total, first) + exact_dot(acc, second)
    row_ref[...] = row


def stats(latent, w_qkv):
    turned = jax.ShapeDtypeStruct((256, 256), bf)
    return pl.pallas_call(
        stats_kernel,
        out_shape=[jax.ShapeDtypeStruct((8, 128), f32), turned, turned],
        in_specs=[VMEM] * 2,
        out_specs=[VMEM] * 3,
        compiler_params=pltpu.CompilerParams(vmem_limit_bytes=16 * 2**20),
    )(latent, w_qkv)


def spread_kernel(row_ref, after_a, after_b, rows_ref):
    rows_ref[...] = jnp.broadcast_to(row_ref[:1], rows_ref.shape)


def spread(row, count, after):
    return pl.pallas_call(
        spread_kernel,
        out_shape=jax.ShapeDtypeStruct((count, 128), f32),
        in_specs=[VMEM] + [HBM] * 2,
        out_specs=VMEM,
    )(row, *after)


def rows_kernel(own, zlow, zhigh, xlow, xhigh, low_ref, high_ref, sems):
    copies = []
    for out, y in ((low_ref, 0), (high_ref, 3)):
        copies += [
            (xlow.at[y], out.at[0]),
            (xhigh.at[y], out.at[3]),
            (own.at[:, y], out.at[1:3, 1:5]),
            (zlow.at[:, y], out.at[1:3, 0]),
            (zhigh.at[:, y], out.at[1:3, 5]),
        ]
    copies = [pltpu.make_async_copy(a, b, sems.at[i]) for i, (a, b) in enumerate(copies)]
    for copy in copies:
        copy.start()
    for copy in copies:
        copy.wait()


def outer_rows(*parts):
    face = jax.ShapeDtypeStruct((4, 6, 64, 256), bf)
    return pl.pallas_call(
        rows_kernel,
        out_shape=[face, face],
        in_specs=[HBM] * 5,
        out_specs=[HBM] * 2,
        scratch_shapes=[pltpu.SemaphoreType.DMA((10,))],
    )(*parts)


def interleave(*stages):
    stages = list(stages)
    while stages:
        for stage in list(stages):
            if next(stage, True):
                stages.remove(stage)


def attend_kernel(ends, edge, limit, *refs):
    if edge:
        own, zlow, zhigh, xlow, xhigh, ylow, yhigh, done, *refs = refs
    else:
        own, zlow, zhigh, xlow, xhigh, *refs = refs
    every, gain, shift_ref, w_qkv, wqT, wvT, wo, bo, out_ref, *refs = refs
    x_ref, k_ref, vt_ref, qbd_ref, om_ref, s_ref, p_ref, m_ref, lists, sems = refs
    copies = [
        (own, x_ref.at[1:3, 1:5, 1:5]),
        (zlow, x_ref.at[1:3, 1:5, 0]),
        (zhigh, x_ref.at[1:3, 1:5, 5]),
        (xlow, x_ref.at[0, 1:5]),
        (xhigh, x_ref.at[3, 1:5]),
    ]
    if edge:
        copies += [(ylow, x_ref.at[:, 0]), (yhigh, x_ref.at[:, 5]), (done, out_ref.at[:, 4:12])]
    copies = [pltpu.make_async_copy(a, b, sems.at[i]) for i, (a, b) in enumerate(copies)]
    for copy in copies:
        copy.start()

    spots = [lax.axis_index(axis) for axis in AXES]
    first = [(spot == 0).astype(jnp.int32) for spot in spots]
    last = [(spot == end).astype(jnp.int32) for spot, end in zip(spots, ends)]

    def place(dim, inner, i):
        out = jnp.where(i == 0, first[dim], jnp.where(i == inner + 1, last[dim], 0))
        return 1 - out, jnp.where(out == 0, i, jnp.where(i == 0, 1, inner))

    entries = 2048.0 * 8.0
    rows = every[...]
    means = jnp.sum(rows, axis=0, keepdims=True) * (1.0 / 256)
    apart = rows - means
    spread = jnp.sum(apart * apart, axis=0, keepdims=True)
    first_of = (iota((128, 256), 0) == iota((128, 256), 1) // 8).astype(f32)
    second_of = (iota((128, 256), 0) == iota((128, 256), 1) // 8 + 32).astype(f32)
    means8, spread8 = jnp.broadcast_to(means, (8, 128)), jnp.broadcast_to(spread, (8, 128))
    mean = exact_dot(means8, first_of)[:1]
    var = (exact_dot(means8, second_of)[:1] * 256 / entries + exact_dot(spread8, first_of)[:1]) * (1.0 / 256)
    mul = lax.rsqrt(var + 1e-06) * gain[...]
    shift = shift_ref[...]

    bys = (0, 3) if edge else (1, 2)

    def sort(i, counts):
        deep, flat = counts
        bx, k, bz = i // 8, (i // 4) % 2, i % 4
        by = k * 3 if edge else k + 1
        spot = bx * 16 + by * 4 + bz
        lists[0, deep] = spot
        lists[1, flat] = spot
        is_deep = (limit[bx, by, bz] != 0).astype(jnp.int32)
        return deep + is_deep, flat + 1 - is_deep

    zero = jnp.int32(0)
    deep, flat = lax.fori_loop(0, 16, sort, (zero, zero))

    own_head = iota((256, 512), 0) // 32 == iota((256, 512), 1) // 64
    diag = iota((128, 256), 0) // 32 == iota((128, 256), 1) // 64
    for copy in copies[:7]:
        copy.wait()

    def normed(cells):
        return ((cells.astype(f32) - mean) * mul + shift).astype(bf)

    lane = iota((1, 256), 1) // 64
    marks = jnp.zeros((1, 256), f32)
    for i in range(4):
        marks = jnp.where(lane == i, place(0, 2, i)[0].astype(f32), marks)
    tick = iota((16, 256), 0) == 0

    def prep_column(c, carry):
        if not edge:
            c = c + 6
        y, z = c // 6, c % 6
        (y_in, y_from), (z_in, z_from) = place(1, 4, y), place(2, 4, z)
        n = normed(
            jnp.concatenate([x_ref[place(0, 2, i)[1], y_from, z_from] for i in range(4)], axis=0)
        )
        k_ref[c] = jnp.dot(n, w_qkv[:, 256:512], preferred_element_type=f32).astype(bf)
        valid = marks * (y_in * z_in).astype(f32)
        vt = lax.dot_general(wvT[...], n, NT, preferred_element_type=f32) * valid
        ones = jnp.where(tick, jnp.broadcast_to(valid, (16, 256)), 0.0)
        for g in range(2):
            t = jnp.concatenate([vt[g * 128 : (g + 1) * 128], ones], axis=0)
            vt_ref[0, c, g] = t[:, :192].astype(bf)
            vt_ref[1, c, g] = pltpu.roll(t, 192, 1)[:, :192].astype(bf)
        return carry

    lax.fori_loop(0, 36 if edge else 24, prep_column, 0, unroll=12)

    def prep_query(i, carry):
        bx, k, bz = i // 8, (i // 4) % 2, i % 4
        by = k * 3 if edge else k + 1
        n = normed(x_ref[bx + 1, by + 1, bz + 1])
        q = lax.dot_general(wqT[...], jnp.concatenate([n] * 4, axis=0), NT, preferred_element_type=f32) * SCALE
        qbd_ref[bx * 16 + by * 4 + bz] = jnp.where(own_head, jnp.concatenate([q, q], axis=1), 0.0).astype(bf)
        return carry

    lax.fori_loop(0, 16, prep_query, 0, unroll=8)

    def columns(i, cols):
        by, bz = (i // 4) % 4, i % 4
        return [(by + dy) * 6 + bz + dz for dy, dz in cols]

    def scores(i, cols):
        rows = pl.ds(pl.multiple_of(i // 16 * 64, 64), 192)
        q, m, spots = qbd_ref[i], None, columns(i, cols)
        for j in range(0, len(cols), 3):
            keys = jnp.concatenate([k_ref[c, rows] for c in spots[j : j + 3]], axis=0)
            s = jnp.dot(keys, q, preferred_element_type=f32)
            s_ref[j * 192 : (j + 3) * 192] = s
            top = jnp.max(s.reshape(-1, 8, 512), axis=0)
            m = top if m is None else jnp.maximum(m, top)
            yield False
        m_ref[...] = jnp.broadcast_to(jnp.max(m, axis=0, keepdims=True), (8, 512))

    def weights(cols):
        top = m_ref[...][:1]
        for j in range(0, len(cols), 3):
            part = slice(j * 192, (j + 3) * 192)
            p_ref[part] = jnp.exp2(s_ref[part] - top).astype(bf)
            yield False

    def mix(i, cols):
        o = [None, None]
        for j, c in enumerate(columns(i, cols)):
            for g in range(2):
                part = jnp.dot(
                    vt_ref[i // 16, c, g],
                    p_ref[j * 192 : (j + 1) * 192, g * 256 : (g + 1) * 256],
                    preferred_element_type=f32,
                )
                o[g] = part if o[g] is None else o[g] + part
            if j % 3 == 2:
                yield False
        for g in range(2):
            om_ref[i, g] = jnp.where(diag, o[g][:128] * (1.0 / o[g][128:129]), 0.0).astype(bf)

    def run(which, count, cols):
        def spot(t):
            return lists[which, jnp.clip(t, 0, count - 1)]

        def step(t, carry):
            interleave(mix(spot(t - 2), cols), weights(cols), scores(spot(t), cols))
            return carry

        @pl.when(count > 0)
        def _():
            interleave(scores(spot(0), cols))
            interleave(weights(cols), scores(spot(1), cols))
            lax.fori_loop(2, count, step, 0)
            interleave(mix(spot(count - 2), cols), weights(cols))
            interleave(mix(spot(count - 1), cols))

    run(0, deep, [(dy, dz) for dz in range(3) for dy in range(3)])
    run(1, flat, [(dy, 1) for dy in range(3)])

    pick = jnp.where(iota((64, 256), 0) == iota((64, 256), 1) % 64, 1.0, 0.0).astype(bf)
    if edge:
        copies[7].wait()

    def finish(i, carry):
        bx, k = i // 2, i % 2
        by = k * 3 if edge else k + 1
        spot = bx * 16 + by * 4
        mixed = [
            jnp.concatenate(
                [lax.dot_general(pick, om_ref[spot + bz, g], NT, preferred_element_type=f32).astype(bf) for g in range(2)],
                axis=1,
            )
            for bz in range(4)
        ]
        out = jnp.dot(jnp.concatenate(mixed, axis=0), wo[...], preferred_element_type=f32) + bo[...]
        y0 = by * 4 if edge else k * 4
        for x in range(4):
            for pair in range(2):
                parts = [out[b * 64 + x * 16 + pair * 8 : b * 64 + x * 16 + pair * 8 + 8] for b in range(4)]
                for which, join in enumerate((low_rows, high_rows)):
                    line = jnp.concatenate([join(parts[0], parts[1]), join(parts[2], parts[3])], axis=0)
                    out_ref[bx * 4 + x, y0 + pair * 2 + which] = line.astype(bf)
        return carry

    lax.fori_loop(0, 4, finish, 0, unroll=2)


def attend(ends, edge, limit, halos, *consts):
    out_y = 16 if edge else 8
    return pl.pallas_call(
        functools.partial(attend_kernel, ends, edge),
        out_shape=jax.ShapeDtypeStruct((8, out_y, 16, 256), bf),
        in_specs=[SMEM] + [HBM] * len(halos) + [VMEM] * len(consts),
        out_specs=VMEM,
        scratch_shapes=[
            pltpu.VMEM((4, 6, 6, 64, 256), bf),
            pltpu.VMEM((36, 256, 256), bf),
            pltpu.VMEM((2, 36, 2, 144, 192), bf),
            pltpu.VMEM((32, 256, 512), bf),
            pltpu.VMEM((32, 2, 128, 256), bf),
            pltpu.VMEM((1728, 512), f32),
            pltpu.VMEM((1728, 512), bf),
            pltpu.VMEM((8, 512), f32),
            pltpu.SMEM((2, 17), jnp.int32),
            pltpu.SemaphoreType.DMA((8,)),
        ],
        compiler_params=pltpu.CompilerParams(vmem_limit_bytes=50 * 2**20),
        cost_estimate=pl.CostEstimate(flops=15 * 10**9, bytes_accessed=8 * 10**6, transcendentals=14 * 10**6),
    )(limit, *halos, *consts)


def swap(low, high, axis):
    count = lax.axis_size(axis)
    up = [(i, i + 1) for i in range(count - 1)]
    down = [(i + 1, i) for i in range(count - 1)]
    return lax.ppermute(high, axis, up), lax.ppermute(low, axis, down)


def on_device(latent, norm_gain, norm_shift, w_qkv, w_out, b_out, depth_limit):
    own, face_low, face_high = arrange(latent)
    zlow, zhigh = swap(face_low, face_high, "gz")

    def deep_layer(x):
        return jnp.concatenate([zlow[x, :, None], own[x], zhigh[x, :, None]], axis=1)

    xsend = deep_layer(0), deep_layer(1)
    xlow, xhigh = swap(*xsend, "gx")
    row, wqT, wvT = stats(latent, w_qkv)
    every = lax.all_to_all(spread(row, lax.axis_size(AXES), xsend), AXES, 0, 0, tiled=True)

    ylow, yhigh = swap(*outer_rows(own, zlow, zhigh, xlow, xhigh), "gy")
    consts = (
        every,
        norm_gain[None],
        norm_shift[None],
        w_qkv,
        wqT,
        wvT,
        w_out,
        b_out[None],
    )
    ends = tuple(lax.axis_size(axis) - 1 for axis in AXES)
    halos = (own, zlow, zhigh, xlow, xhigh)
    middle = attend(ends, False, depth_limit, halos, *consts)
    return attend(ends, True, depth_limit, halos + (ylow, yhigh, middle), *consts)


def solution(mesh):
    placed = (P("gx", "gy", "gz", None), P(), P(), P(), P(), P(), P("gx", "gy", "gz"))
    return jax.shard_map(
        on_device, mesh=mesh, in_specs=placed, out_specs=P("gx", "gy", "gz", None), check_vma=False
    )
```

```python
import functools

import jax
import jax.numpy as jnp
import numpy as np
from jax import lax
from jax.experimental import pallas as pl
from jax.experimental.pallas import tpu as pltpu
from jax.sharding import PartitionSpec as P

GROUPS = 32
AXES = ("gx", "gy", "gz")
f32, bf = jnp.float32, jnp.bfloat16
NT = (((1,), (1,)), ((), ()))
SCALE = float(np.log2(np.e) / np.sqrt(32.0))
VMEM = pl.BlockSpec(memory_space=pltpu.VMEM)
SMEM = pl.BlockSpec(memory_space=pltpu.SMEM)
HBM = pl.BlockSpec(memory_space=pl.ANY)


def iota(shape, dim):
    return lax.broadcasted_iota(jnp.int32, shape, dim)


def exact_dot(a, b):
    return jnp.dot(a, b, precision=lax.Precision.HIGHEST, preferred_element_type=f32)


def low_rows(a, b):
    return jnp.where(iota(a.shape, 0) < 4, a, pltpu.roll(b, 4, 0))


def high_rows(a, b):
    return jnp.where(iota(a.shape, 0) < 4, pltpu.roll(a, 4, 0), b)


def arrange_kernel(x_ref, own0_ref, own1_ref, low_ref, high_ref):
    for bx in range(2):
        for by in range(4):

            def plane(x, carry, bx=bx, by=by):
                for half in range(2):
                    lows, highs = [], []
                    for pair in range(2):
                        a, b = [
                            x_ref[bx * 4 + x, by * 4 + pair * 2 + k, half * 8 : half * 8 + 8].astype(f32)
                            for k in range(2)
                        ]
                        lows.append(low_rows(a, b))
                        highs.append(high_rows(a, b))
                    rows = pl.ds(pl.multiple_of(x * 16, 16), 16)
                    for k, parts in enumerate((lows, highs)):
                        piece = jnp.concatenate(parts, axis=0).astype(bf)
                        (own0_ref, own1_ref)[bx][by, half * 2 + k, rows] = piece
                        if (half, k) == (0, 0):
                            low_ref[bx, by, rows] = piece
                        if (half, k) == (1, 1):
                            high_ref[bx, by, rows] = piece
                return carry

            lax.fori_loop(0, 4, plane, 0, unroll=True)


def arrange(latent):
    return pl.pallas_call(
        arrange_kernel,
        out_shape=[
            jax.ShapeDtypeStruct((4, 4, 64, 256), bf),
            jax.ShapeDtypeStruct((4, 4, 64, 256), bf),
            jax.ShapeDtypeStruct((2, 4, 64, 256), bf),
            jax.ShapeDtypeStruct((2, 4, 64, 256), bf),
        ],
        in_specs=[VMEM],
        out_specs=[VMEM] * 4,
        compiler_params=pltpu.CompilerParams(vmem_limit_bytes=24 * 2**20),
    )(latent)


def stats_kernel(x_ref, row_ref):
    entries = 2048 * 8

    def sums(i, acc):
        return acc + jnp.sum(x_ref[i].astype(f32).reshape(32, 8, 256), axis=0)

    zeros = jnp.zeros((8, 256), f32)
    total = lax.fori_loop(0, 8, sums, zeros)
    total = jnp.broadcast_to(jnp.sum(total, axis=0, keepdims=True), (8, 256)) * (1.0 / entries)
    same = (iota((256, 256), 0) // 8 == iota((256, 256), 1) // 8).astype(f32)
    mean = exact_dot(total, same)

    def squares(i, acc):
        cells = x_ref[i].astype(f32) - mean[:1][None]
        return acc + jnp.sum((cells * cells).reshape(32, 8, 256), axis=0)

    acc = lax.fori_loop(0, 8, squares, zeros)
    acc = jnp.broadcast_to(jnp.sum(acc, axis=0, keepdims=True), (8, 256))
    first = (iota((256, 128), 0) // 8 == iota((256, 128), 1)).astype(f32)
    second = (iota((256, 128), 0) // 8 + 32 == iota((256, 128), 1)).astype(f32)
    row = exact_dot(total, first) + exact_dot(acc, second)
    row_ref[...] = row


def stats(latent):
    return pl.pallas_call(
        stats_kernel,
        out_shape=jax.ShapeDtypeStruct((8, 128), f32),
        in_specs=[VMEM],
        out_specs=VMEM,
        compiler_params=pltpu.CompilerParams(vmem_limit_bytes=16 * 2**20),
    )(latent)


def edges_kernel(entries, held_ref, zlow, zhigh, low_ref, high_ref, rows_ref):
    for x, out in enumerate((low_ref, high_ref)):
        out[0], out[1] = zlow[x], zhigh[x]
    held = held_ref[...]
    share = 1.0 / held.shape[0]
    total = jnp.sum(held, axis=0, keepdims=True)
    apart = held - total * share
    spread = jnp.sum(apart * apart, axis=0, keepdims=True) * (entries / 8)
    total, spread = jnp.broadcast_to(total, (8, 128)), jnp.broadcast_to(spread, (8, 128))
    lane = iota((8, 128), 1)
    merged = jnp.where(lane < 64, total * (1.0 / 8) + pltpu.roll(spread, 32, 1), 0.0)
    merged = jnp.where(lane < 32, total * share, merged)
    rows_ref[...] = jnp.broadcast_to(merged[:1], rows_ref.shape)


def y_faces_kernel(own0, own1, zlow, zhigh, xlow, xhigh, xzlow, xzhigh, low_ref, high_ref):
    for y, out in ((0, low_ref), (3, high_ref)):
        for x, (inner, zhalo) in enumerate(((xlow, xzlow), (own0, None), (own1, None), (xhigh, xzhigh))):
            out[x, 1:5] = inner[y]
            out[x, 0] = zlow[x - 1, y] if zhalo is None else zhalo[0, y]
            out[x, 5] = zhigh[x - 1, y] if zhalo is None else zhalo[1, y]


def faces(kernel, shape, parts, *more):
    face = jax.ShapeDtypeStruct(shape, bf)
    return pl.pallas_call(
        kernel,
        out_shape=[face, face, *more],
        in_specs=[VMEM] * len(parts),
        out_specs=[VMEM] * (2 + len(more)),
        compiler_params=pltpu.CompilerParams(vmem_limit_bytes=16 * 2**20),
    )(*parts)


def interleave(*stages):
    stages = list(stages)
    while stages:
        for stage in list(stages):
            if next(stage, True):
                stages.remove(stage)


def attend_kernel(ends, edge, limit, *refs):
    halos, refs = (refs[:11], refs[11:]) if edge else (refs[:8], refs[8:])
    own0, own1, zlow, zhigh, xlow, xhigh, xzlow, xzhigh, *late = halos
    consts, (out_ref, *refs) = refs[:6], refs[6:]
    x_ref, k_ref, vt_ref, qbd_ref, om_ref, s_ref, p_ref, m_ref, lists, sems, wqT, wvT, *held = refs
    every, gain, shift_ref, w_qkv, wo, bo = held
    copies = list(zip(consts, held)) + [
        (own0, x_ref.at[1, 1:5, 1:5]),
        (own1, x_ref.at[2, 1:5, 1:5]),
        (zlow, x_ref.at[1:3, 1:5, 0]),
        (zhigh, x_ref.at[1:3, 1:5, 5]),
        (xlow, x_ref.at[0, 1:5, 1:5]),
        (xhigh, x_ref.at[3, 1:5, 1:5]),
        (xzlow.at[0], x_ref.at[0, 1:5, 0]),
        (xzlow.at[1], x_ref.at[0, 1:5, 5]),
        (xzhigh.at[0], x_ref.at[3, 1:5, 0]),
        (xzhigh.at[1], x_ref.at[3, 1:5, 5]),
    ]
    if edge:
        copies += list(zip(late, (x_ref.at[:, 0], x_ref.at[:, 5], out_ref.at[:, 4:12])))
    copies = [pltpu.make_async_copy(a, b, sems.at[i]) for i, (a, b) in enumerate(copies)]
    for copy in copies:
        copy.start()

    spots = [lax.axis_index(axis) for axis in AXES]
    first = [(spot == 0).astype(jnp.int32) for spot in spots]
    last = [(spot == end).astype(jnp.int32) for spot, end in zip(spots, ends)]

    def place(dim, inner, i):
        out = jnp.where(i == 0, first[dim], jnp.where(i == inner + 1, last[dim], 0))
        return 1 - out, jnp.where(out == 0, i, jnp.where(i == 0, 1, inner))

    for copy in copies[:4]:
        copy.wait()
    wqT[...] = w_qkv[:, :256].astype(f32).T.astype(bf)
    wvT[...] = w_qkv[:, 512:].astype(f32).T.astype(bf)
    held_by = every.shape[0]
    entries = 2048.0 * 8.0 * (256 // held_by)
    rows = every[...]
    means = jnp.sum(rows, axis=0, keepdims=True) * (1.0 / held_by)
    apart = rows - means
    spread = jnp.sum(apart * apart, axis=0, keepdims=True)
    first_of = (iota((128, 256), 0) == iota((128, 256), 1) // 8).astype(f32)
    second_of = (iota((128, 256), 0) == iota((128, 256), 1) // 8 + 32).astype(f32)
    means8, spread8 = jnp.broadcast_to(means, (8, 128)), jnp.broadcast_to(spread, (8, 128))
    mean = exact_dot(means8, first_of)[:1]
    var = (exact_dot(means8, second_of)[:1] * (held_by / entries) + exact_dot(spread8, first_of)[:1]) * (1.0 / held_by)
    mul = lax.rsqrt(var + 1e-06) * gain[...]
    shift = shift_ref[...]

    bys = (0, 3) if edge else (1, 2)

    def sort(i, counts):
        deep, flat = counts
        bx, k, bz = i // 8, (i // 4) % 2, i % 4
        by = k * 3 if edge else k + 1
        spot = bx * 16 + by * 4 + bz
        lists[0, deep] = spot
        lists[1, flat] = spot
        is_deep = (limit[bx, by, bz] != 0).astype(jnp.int32)
        return deep + is_deep, flat + 1 - is_deep

    zero = jnp.int32(0)
    deep, flat = lax.fori_loop(0, 16, sort, (zero, zero))

    own_head = iota((256, 512), 0) // 32 == iota((256, 512), 1) // 64
    diag = iota((128, 256), 0) // 32 == iota((128, 256), 1) // 64
    for copy in copies[4 : 18 if edge else 16]:
        copy.wait()

    def normed(cells):
        return ((cells.astype(f32) - mean) * mul + shift).astype(bf)

    lane = iota((1, 256), 1) // 64
    marks = jnp.zeros((1, 256), f32)
    for i in range(4):
        marks = jnp.where(lane == i, place(0, 2, i)[0].astype(f32), marks)
    tick = iota((16, 256), 0) == 0

    def prep_column(c, carry):
        if not edge:
            c = c + 6
        y, z = c // 6, c % 6
        (y_in, y_from), (z_in, z_from) = place(1, 4, y), place(2, 4, z)
        n = normed(
            jnp.concatenate([x_ref[place(0, 2, i)[1], y_from, z_from] for i in range(4)], axis=0)
        )
        k_ref[c] = jnp.dot(n, w_qkv[:, 256:512], preferred_element_type=f32).astype(bf)
        valid = marks * (y_in * z_in).astype(f32)
        vt = lax.dot_general(wvT[...], n, NT, preferred_element_type=f32) * valid
        ones = jnp.where(tick, jnp.broadcast_to(valid, (16, 256)), 0.0)
        for g in range(2):
            t = jnp.concatenate([vt[g * 128 : (g + 1) * 128], ones], axis=0)
            vt_ref[0, c, g] = t[:, :192].astype(bf)
            vt_ref[1, c, g] = pltpu.roll(t, 192, 1)[:, :192].astype(bf)
        return carry

    lax.fori_loop(0, 36 if edge else 24, prep_column, 0, unroll=12)

    def prep_query(i, carry):
        bx, k, bz = i // 8, (i // 4) % 2, i % 4
        by = k * 3 if edge else k + 1
        n = normed(x_ref[bx + 1, by + 1, bz + 1])
        q = lax.dot_general(wqT[...], jnp.concatenate([n] * 4, axis=0), NT, preferred_element_type=f32) * SCALE
        qbd_ref[bx * 16 + by * 4 + bz] = jnp.where(own_head, jnp.concatenate([q, q], axis=1), 0.0).astype(bf)
        return carry

    lax.fori_loop(0, 16, prep_query, 0, unroll=8)

    def columns(i, cols):
        by, bz = (i // 4) % 4, i % 4
        return [(by + dy) * 6 + bz + dz for dy, dz in cols]

    def scores(i, cols):
        rows = pl.ds(pl.multiple_of(i // 16 * 64, 64), 192)
        q, m, spots = qbd_ref[i], None, columns(i, cols)
        for j in range(0, len(cols), 3):
            keys = jnp.concatenate([k_ref[c, rows] for c in spots[j : j + 3]], axis=0)
            s = jnp.dot(keys, q, preferred_element_type=f32)
            s_ref[j * 192 : (j + 3) * 192] = s
            top = jnp.max(s.reshape(-1, 8, 512), axis=0)
            m = top if m is None else jnp.maximum(m, top)
            yield False
        m_ref[...] = jnp.broadcast_to(jnp.max(m, axis=0, keepdims=True), (8, 512))

    def weights(cols):
        top = m_ref[...][:1]
        for j in range(0, len(cols), 3):
            part = slice(j * 192, (j + 3) * 192)
            p_ref[part] = jnp.exp2(s_ref[part] - top).astype(bf)
            yield False

    def mix(i, cols):
        o = [None, None]
        for j, c in enumerate(columns(i, cols)):
            for g in range(2):
                part = jnp.dot(
                    vt_ref[i // 16, c, g],
                    p_ref[j * 192 : (j + 1) * 192, g * 256 : (g + 1) * 256],
                    preferred_element_type=f32,
                )
                o[g] = part if o[g] is None else o[g] + part
            if j % 3 == 2:
                yield False
        for g in range(2):
            om_ref[i, g] = jnp.where(diag, o[g][:128] * (1.0 / o[g][128:129]), 0.0).astype(bf)

    def run(which, count, cols):
        def spot(t):
            return lists[which, jnp.clip(t, 0, count - 1)]

        def step(t, carry):
            interleave(mix(spot(t - 2), cols), weights(cols), scores(spot(t), cols))
            return carry

        @pl.when(count > 0)
        def _():
            interleave(scores(spot(0), cols))
            interleave(weights(cols), scores(spot(1), cols))
            lax.fori_loop(2, count, step, 0)
            interleave(mix(spot(count - 2), cols), weights(cols))
            interleave(mix(spot(count - 1), cols))

    run(0, deep, [(dy, dz) for dz in range(3) for dy in range(3)])
    run(1, flat, [(dy, 1) for dy in range(3)])

    pick = jnp.where(iota((64, 256), 0) == iota((64, 256), 1) % 64, 1.0, 0.0).astype(bf)
    if edge:
        copies[18].wait()

    def finish(i, carry):
        bx, k = i // 2, i % 2
        by = k * 3 if edge else k + 1
        spot = bx * 16 + by * 4
        mixed = [
            jnp.concatenate(
                [lax.dot_general(pick, om_ref[spot + bz, g], NT, preferred_element_type=f32).astype(bf) for g in range(2)],
                axis=1,
            )
            for bz in range(4)
        ]
        out = jnp.dot(jnp.concatenate(mixed, axis=0), wo[...], preferred_element_type=f32) + bo[...]
        y0 = by * 4 if edge else k * 4
        for x in range(4):
            for pair in range(2):
                parts = [out[b * 64 + x * 16 + pair * 8 : b * 64 + x * 16 + pair * 8 + 8] for b in range(4)]
                for which, join in enumerate((low_rows, high_rows)):
                    line = jnp.concatenate([join(parts[0], parts[1]), join(parts[2], parts[3])], axis=0)
                    out_ref[bx * 4 + x, y0 + pair * 2 + which] = line.astype(bf)
        return carry

    lax.fori_loop(0, 4, finish, 0, unroll=2)


def attend(ends, edge, limit, halos, *consts):
    out_y = 16 if edge else 8
    return pl.pallas_call(
        functools.partial(attend_kernel, ends, edge),
        out_shape=jax.ShapeDtypeStruct((8, out_y, 16, 256), bf),
        in_specs=[SMEM] + [HBM] * (len(halos) + len(consts)),
        out_specs=VMEM,
        scratch_shapes=[
            pltpu.VMEM((4, 6, 6, 64, 256), bf),
            pltpu.VMEM((36, 256, 256), bf),
            pltpu.VMEM((2, 36, 2, 144, 192), bf),
            pltpu.VMEM((32, 256, 512), bf),
            pltpu.VMEM((32, 2, 128, 256), bf),
            pltpu.VMEM((1728, 512), f32),
            pltpu.VMEM((1728, 512), bf),
            pltpu.VMEM((8, 512), f32),
            pltpu.SMEM((2, 17), jnp.int32),
            pltpu.SemaphoreType.DMA((19,)),
            pltpu.VMEM((256, 256), bf),
            pltpu.VMEM((256, 256), bf),
        ]
        + [pltpu.VMEM(const.shape, const.dtype) for const in consts],
        compiler_params=pltpu.CompilerParams(vmem_limit_bytes=50 * 2**20),
        cost_estimate=pl.CostEstimate(flops=15 * 10**9, bytes_accessed=8 * 10**6, transcendentals=14 * 10**6),
    )(limit, *halos, *consts)


def swap(low, high, axis):
    count = lax.axis_size(axis)
    up = [(i, i + 1) for i in range(count - 1)]
    down = [(i + 1, i) for i in range(count - 1)]
    return lax.ppermute(high, axis, up), lax.ppermute(low, axis, down)


def on_device(latent, norm_gain, norm_shift, w_qkv, w_out, b_out, depth_limit):
    own0, own1, face_low, face_high = arrange(latent)
    zlow, zhigh = swap(face_low, face_high, "gz")
    xlow, xhigh = swap(own0, own1, "gx")
    held, step = stats(latent), 1
    while step < lax.axis_size("gy"):
        pairs = [(i, i ^ step) for i in range(lax.axis_size("gy"))]
        held = jnp.concatenate([held, lax.ppermute(held, "gy", pairs)], axis=0)
        step *= 2
    rest = ("gx", "gz")
    rows = jax.ShapeDtypeStruct((lax.axis_size(rest), 128), f32)
    kernel = functools.partial(edges_kernel, float(latent.size // 32))
    *edges, rows = faces(kernel, (2, 4, 64, 256), (held, zlow, zhigh), rows)
    xzlow, xzhigh = swap(*edges, "gx")
    every = lax.all_to_all(rows, rest, 0, 0, tiled=True)
    near = (own0, own1, zlow, zhigh, xlow, xhigh, xzlow, xzhigh)
    ylow, yhigh = swap(*faces(y_faces_kernel, (4, 6, 64, 256), near), "gy")
    consts = (
        every,
        norm_gain[None],
        norm_shift[None],
        w_qkv,
        w_out,
        b_out[None],
    )
    ends = tuple(lax.axis_size(axis) - 1 for axis in AXES)
    middle = attend(ends, False, depth_limit, near, *consts)
    return attend(ends, True, depth_limit, near + (ylow, yhigh, middle), *consts)


def solution(mesh):
    placed = (P("gx", "gy", "gz", None), P(), P(), P(), P(), P(), P("gx", "gy", "gz"))
    return jax.shard_map(
        on_device, mesh=mesh, in_specs=placed, out_specs=P("gx", "gy", "gz", None), check_vma=False
    )
```

```python
import functools

import jax
import jax.numpy as jnp
import numpy as np
from jax import lax
from jax.experimental import pallas as pl
from jax.experimental.pallas import tpu as pltpu
from jax.sharding import PartitionSpec as P

GROUPS = 32
AXES = ("gx", "gy", "gz")
f32, bf = jnp.float32, jnp.bfloat16
NT = (((1,), (1,)), ((), ()))
SCALE = float(np.log2(np.e) / np.sqrt(32.0))
VMEM = pl.BlockSpec(memory_space=pltpu.VMEM)
SMEM = pl.BlockSpec(memory_space=pltpu.SMEM)
HBM = pl.BlockSpec(memory_space=pl.ANY)


def iota(shape, dim):
    return lax.broadcasted_iota(jnp.int32, shape, dim)


def exact_dot(a, b):
    return jnp.dot(a, b, precision=lax.Precision.HIGHEST, preferred_element_type=f32)


def low_rows(a, b):
    return jnp.where(iota(a.shape, 0) < 4, a, pltpu.roll(b, 4, 0))


def high_rows(a, b):
    return jnp.where(iota(a.shape, 0) < 4, pltpu.roll(a, 4, 0), b)


def block_rows(x_ref, x, y, half):
    lows, highs = [], []
    for pair in range(2):
        a, b = [x_ref[x, y + pair * 2 + k, half * 8 : half * 8 + 8].astype(f32) for k in range(2)]
        lows.append(low_rows(a, b))
        highs.append(high_rows(a, b))
    return [jnp.concatenate(parts, axis=0).astype(bf) for parts in (lows, highs)]


def z_faces_kernel(x_ref, low_ref, high_ref):
    for bx in range(2):
        for by in range(4):
            for x in range(4):
                rows = slice(x * 16, x * 16 + 16)
                low_ref[bx, by, rows] = block_rows(x_ref, bx * 4 + x, by * 4, 0)[0]
                high_ref[bx, by, rows] = block_rows(x_ref, bx * 4 + x, by * 4, 1)[1]


def z_faces(latent):
    face = jax.ShapeDtypeStruct((2, 4, 64, 256), bf)
    return pl.pallas_call(
        z_faces_kernel,
        out_shape=[face, face],
        in_specs=[VMEM],
        out_specs=[VMEM] * 2,
        compiler_params=pltpu.CompilerParams(vmem_limit_bytes=16 * 2**20),
    )(latent)


def arrange_kernel(x_ref, own0_ref, own1_ref, row_ref):
    for bx, own_ref in enumerate((own0_ref, own1_ref)):
        for by in range(4):
            for x in range(4):
                for half in range(2):
                    for k, piece in enumerate(block_rows(x_ref, bx * 4 + x, by * 4, half)):
                        own_ref[by, half * 2 + k, x * 16 : x * 16 + 16] = piece
    entries = 2048 * 8

    def sums(i, acc):
        return acc + jnp.sum(x_ref[i].astype(f32).reshape(32, 8, 256), axis=0)

    zeros = jnp.zeros((8, 256), f32)
    total = lax.fori_loop(0, 8, sums, zeros)
    total = jnp.broadcast_to(jnp.sum(total, axis=0, keepdims=True), (8, 256)) * (1.0 / entries)
    same = (iota((256, 256), 0) // 8 == iota((256, 256), 1) // 8).astype(f32)
    mean = exact_dot(total, same)

    def squares(i, acc):
        cells = x_ref[i].astype(f32) - mean[:1][None]
        return acc + jnp.sum((cells * cells).reshape(32, 8, 256), axis=0)

    acc = lax.fori_loop(0, 8, squares, zeros)
    acc = jnp.broadcast_to(jnp.sum(acc, axis=0, keepdims=True), (8, 256))
    first = (iota((256, 128), 0) // 8 == iota((256, 128), 1)).astype(f32)
    second = (iota((256, 128), 0) // 8 + 32 == iota((256, 128), 1)).astype(f32)
    row = exact_dot(total, first) + exact_dot(acc, second)
    row_ref[...] = jnp.broadcast_to(row[:1], row_ref.shape)


def arrange(latent):
    own = jax.ShapeDtypeStruct((4, 4, 64, 256), bf)
    return pl.pallas_call(
        arrange_kernel,
        out_shape=[own, own, jax.ShapeDtypeStruct((8, 128), f32)],
        in_specs=[VMEM],
        out_specs=[VMEM] * 3,
        compiler_params=pltpu.CompilerParams(vmem_limit_bytes=16 * 2**20),
    )(latent)


def edges_kernel(entries, held_ref, zlow, zhigh, low_ref, high_ref, rows_ref):
    for x, out in enumerate((low_ref, high_ref)):
        out[0], out[1] = zlow[x], zhigh[x]
    held = held_ref[...]
    share = 1.0 / held.shape[0]
    total = jnp.sum(held, axis=0, keepdims=True)
    apart = held - total * share
    spread = jnp.sum(apart * apart, axis=0, keepdims=True) * (entries / 8)
    total, spread = jnp.broadcast_to(total, (8, 128)), jnp.broadcast_to(spread, (8, 128))
    lane = iota((8, 128), 1)
    merged = jnp.where(lane < 64, total * (1.0 / 8) + pltpu.roll(spread, 32, 1), 0.0)
    merged = jnp.where(lane < 32, total * share, merged)
    rows_ref[...] = jnp.broadcast_to(merged[:1], rows_ref.shape)


def y_faces_kernel(own0, own1, zlow, zhigh, xlow, xhigh, xzlow, xzhigh, low_ref, high_ref):
    for y, out in ((0, low_ref), (3, high_ref)):
        for x, (inner, zhalo) in enumerate(((xlow, xzlow), (own0, None), (own1, None), (xhigh, xzhigh))):
            out[x, 1:5] = inner[y]
            out[x, 0] = zlow[x - 1, y] if zhalo is None else zhalo[0, y]
            out[x, 5] = zhigh[x - 1, y] if zhalo is None else zhalo[1, y]


def faces(kernel, shape, parts, *more):
    face = jax.ShapeDtypeStruct(shape, bf)
    return pl.pallas_call(
        kernel,
        out_shape=[face, face, *more],
        in_specs=[VMEM] * len(parts),
        out_specs=[VMEM] * (2 + len(more)),
        compiler_params=pltpu.CompilerParams(vmem_limit_bytes=16 * 2**20),
    )(*parts)


def interleave(*stages):
    stages = list(stages)
    while stages:
        for stage in list(stages):
            if next(stage, True):
                stages.remove(stage)


def attend_kernel(ends, edge, limit, *refs):
    halos, refs = (refs[:11], refs[11:]) if edge else (refs[:8], refs[8:])
    own0, own1, zlow, zhigh, xlow, xhigh, xzlow, xzhigh, *late = halos
    consts, (out_ref, *refs) = refs[:6], refs[6:]
    x_ref, k_ref, vt_ref, qbd_ref, om_ref, s_ref, p_ref, m_ref, lists, sems, wqT, wvT, *held = refs
    every, gain, shift_ref, w_qkv, wo, bo = held
    copies = list(zip(consts, held)) + [
        (own0, x_ref.at[1, 1:5, 1:5]),
        (own1, x_ref.at[2, 1:5, 1:5]),
        (zlow, x_ref.at[1:3, 1:5, 0]),
        (zhigh, x_ref.at[1:3, 1:5, 5]),
        (xlow, x_ref.at[0, 1:5, 1:5]),
        (xhigh, x_ref.at[3, 1:5, 1:5]),
        (xzlow.at[0], x_ref.at[0, 1:5, 0]),
        (xzlow.at[1], x_ref.at[0, 1:5, 5]),
        (xzhigh.at[0], x_ref.at[3, 1:5, 0]),
        (xzhigh.at[1], x_ref.at[3, 1:5, 5]),
    ]
    if edge:
        done = late.pop()
        copies += list(zip(late, (x_ref.at[:, 0], x_ref.at[:, 5])))
    copies = [pltpu.make_async_copy(a, b, sems.at[i]) for i, (a, b) in enumerate(copies)]
    for copy in copies:
        copy.start()

    spots = [lax.axis_index(axis) for axis in AXES]
    first = [(spot == 0).astype(jnp.int32) for spot in spots]
    last = [(spot == end).astype(jnp.int32) for spot, end in zip(spots, ends)]

    def place(dim, inner, i):
        out = jnp.where(i == 0, first[dim], jnp.where(i == inner + 1, last[dim], 0))
        return 1 - out, jnp.where(out == 0, i, jnp.where(i == 0, 1, inner))

    for copy in copies[:4]:
        copy.wait()
    wqT[...] = w_qkv[:, :256].astype(f32).T.astype(bf)
    wvT[...] = w_qkv[:, 512:].astype(f32).T.astype(bf)
    held_by = every.shape[0]
    entries = 2048.0 * 8.0 * (256 // held_by)
    rows = every[...]
    means = jnp.sum(rows, axis=0, keepdims=True) * (1.0 / held_by)
    apart = rows - means
    spread = jnp.sum(apart * apart, axis=0, keepdims=True)
    first_of = (iota((128, 256), 0) == iota((128, 256), 1) // 8).astype(f32)
    second_of = (iota((128, 256), 0) == iota((128, 256), 1) // 8 + 32).astype(f32)
    means8, spread8 = jnp.broadcast_to(means, (8, 128)), jnp.broadcast_to(spread, (8, 128))
    mean = exact_dot(means8, first_of)[:1]
    var = (exact_dot(means8, second_of)[:1] * (held_by / entries) + exact_dot(spread8, first_of)[:1]) * (1.0 / held_by)
    mul = lax.rsqrt(var + 1e-06) * gain[...]
    shift = shift_ref[...]

    bys = (0, 3) if edge else (1, 2)

    def sort(i, counts):
        deep, flat = counts
        bx, k, bz = i // 8, (i // 4) % 2, i % 4
        by = k * 3 if edge else k + 1
        spot = bx * 16 + by * 4 + bz
        lists[0, deep] = spot
        lists[1, flat] = spot
        is_deep = (limit[bx, by, bz] != 0).astype(jnp.int32)
        return deep + is_deep, flat + 1 - is_deep

    zero = jnp.int32(0)
    deep, flat = lax.fori_loop(0, 16, sort, (zero, zero))

    own_head = iota((256, 512), 0) // 32 == iota((256, 512), 1) // 64
    diag = iota((128, 256), 0) // 32 == iota((128, 256), 1) // 64
    for copy in copies[4:16]:
        copy.wait()

    def normed(cells):
        return ((cells.astype(f32) - mean) * mul + shift).astype(bf)

    lane = iota((1, 256), 1) // 64
    marks = jnp.zeros((1, 256), f32)
    for i in range(4):
        marks = jnp.where(lane == i, place(0, 2, i)[0].astype(f32), marks)
    tick = iota((16, 256), 0) == 0

    def prep_column(c, carry):
        y, z = c // 6, c % 6
        (y_in, y_from), (z_in, z_from) = place(1, 4, y), place(2, 4, z)
        n = normed(
            jnp.concatenate([x_ref[place(0, 2, i)[1], y_from, z_from] for i in range(4)], axis=0)
        )
        k_ref[c] = jnp.dot(n, w_qkv[:, 256:512], preferred_element_type=f32).astype(bf)
        valid = marks * (y_in * z_in).astype(f32)
        vt = lax.dot_general(wvT[...], n, NT, preferred_element_type=f32) * valid
        ones = jnp.where(tick, jnp.broadcast_to(valid, (16, 256)), 0.0)
        for g in range(2):
            t = jnp.concatenate([vt[g * 128 : (g + 1) * 128], ones], axis=0)
            vt_ref[0, c, g] = t[:, :192].astype(bf)
            vt_ref[1, c, g] = pltpu.roll(t, 192, 1)[:, :192].astype(bf)
        return carry

    lax.fori_loop(6, 30, prep_column, 0, unroll=24)

    def prep_query(i, carry):
        bx, k, bz = i // 8, (i // 4) % 2, i % 4
        by = k * 3 if edge else k + 1
        n = normed(x_ref[bx + 1, by + 1, bz + 1])
        q = lax.dot_general(wqT[...], jnp.concatenate([n] * 4, axis=0), NT, preferred_element_type=f32) * SCALE
        qbd_ref[bx * 16 + by * 4 + bz] = jnp.where(own_head, jnp.concatenate([q, q], axis=1), 0.0).astype(bf)
        return carry

    lax.fori_loop(0, 16, prep_query, 0, unroll=16)
    if edge:
        for copy in copies[16:]:
            copy.wait()
        lax.fori_loop(0, 12, lambda t, carry: prep_column(jnp.where(t < 6, t, t + 24), carry), 0, unroll=12)

    def columns(i, cols):
        by, bz = (i // 4) % 4, i % 4
        return [(by + dy) * 6 + bz + dz for dy, dz in cols]

    def scores(i, cols):
        rows = pl.ds(pl.multiple_of(i // 16 * 64, 64), 192)
        q, m, spots = qbd_ref[i], None, columns(i, cols)
        for j in range(0, len(cols), 3):
            keys = jnp.concatenate([k_ref[c, rows] for c in spots[j : j + 3]], axis=0)
            s = jnp.dot(keys, q, preferred_element_type=f32)
            s_ref[j * 192 : (j + 3) * 192] = s
            top = jnp.max(s.reshape(-1, 8, 512), axis=0)
            m = top if m is None else jnp.maximum(m, top)
            yield False
        m_ref[...] = jnp.broadcast_to(jnp.max(m, axis=0, keepdims=True), (8, 512))

    def weights(cols):
        top = m_ref[...][:1]
        for j in range(0, len(cols), 3):
            part = slice(j * 192, (j + 3) * 192)
            p_ref[part] = jnp.exp2(s_ref[part] - top).astype(bf)
            yield False

    def mix(i, cols):
        o = [None, None]
        for j, c in enumerate(columns(i, cols)):
            for g in range(2):
                part = jnp.dot(
                    vt_ref[i // 16, c, g],
                    p_ref[j * 192 : (j + 1) * 192, g * 256 : (g + 1) * 256],
                    preferred_element_type=f32,
                )
                o[g] = part if o[g] is None else o[g] + part
            if j % 3 == 2:
                yield False
        for g in range(2):
            om_ref[i, g] = jnp.where(diag, o[g][:128] * (1.0 / o[g][128:129]), 0.0).astype(bf)

    def run(which, count, cols):
        def spot(t):
            return lists[which, jnp.clip(t, 0, count - 1)]

        def step(t, carry):
            interleave(mix(spot(t - 2), cols), weights(cols), scores(spot(t), cols))
            return carry

        @pl.when(count > 0)
        def _():
            interleave(scores(spot(0), cols))
            interleave(weights(cols), scores(spot(1), cols))
            lax.fori_loop(2, count, step, 0)
            interleave(mix(spot(count - 2), cols), weights(cols))
            interleave(mix(spot(count - 1), cols))

    run(0, deep, [(dy, dz) for dz in range(3) for dy in range(3)])
    run(1, flat, [(dy, 1) for dy in range(3)])

    pick = jnp.where(iota((64, 256), 0) == iota((64, 256), 1) % 64, 1.0, 0.0).astype(bf)
    if edge:
        out_ref[:, 4:12] = done[...]

    def finish(i, carry):
        bx, k = i // 2, i % 2
        by = k * 3 if edge else k + 1
        spot = bx * 16 + by * 4
        mixed = [
            jnp.concatenate(
                [lax.dot_general(pick, om_ref[spot + bz, g], NT, preferred_element_type=f32).astype(bf) for g in range(2)],
                axis=1,
            )
            for bz in range(4)
        ]
        out = jnp.dot(jnp.concatenate(mixed, axis=0), wo[...], preferred_element_type=f32) + bo[...]
        y0 = by * 4 if edge else k * 4
        for x in range(4):
            for pair in range(2):
                parts = [out[b * 64 + x * 16 + pair * 8 : b * 64 + x * 16 + pair * 8 + 8] for b in range(4)]
                for which, join in enumerate((low_rows, high_rows)):
                    line = jnp.concatenate([join(parts[0], parts[1]), join(parts[2], parts[3])], axis=0)
                    out_ref[bx * 4 + x, y0 + pair * 2 + which] = line.astype(bf)
        return carry

    lax.fori_loop(0, 4, finish, 0, unroll=4)


def attend(ends, edge, limit, halos, *consts):
    out_y = 16 if edge else 8
    return pl.pallas_call(
        functools.partial(attend_kernel, ends, edge),
        out_shape=jax.ShapeDtypeStruct((8, out_y, 16, 256), bf),
        in_specs=[SMEM] + [VMEM if half.shape[0] == 8 else HBM for half in halos] + [HBM] * len(consts),
        out_specs=VMEM,
        scratch_shapes=[
            pltpu.VMEM((4, 6, 6, 64, 256), bf),
            pltpu.VMEM((36, 256, 256), bf),
            pltpu.VMEM((2, 36, 2, 144, 192), bf),
            pltpu.VMEM((32, 256, 512), bf),
            pltpu.VMEM((32, 2, 128, 256), bf),
            pltpu.VMEM((1728, 512), f32),
            pltpu.VMEM((1728, 512), bf),
            pltpu.VMEM((8, 512), f32),
            pltpu.SMEM((2, 17), jnp.int32),
            pltpu.SemaphoreType.DMA((18,)),
            pltpu.VMEM((256, 256), bf),
            pltpu.VMEM((256, 256), bf),
        ]
        + [pltpu.VMEM(const.shape, const.dtype) for const in consts],
        compiler_params=pltpu.CompilerParams(vmem_limit_bytes=50 * 2**20),
        cost_estimate=pl.CostEstimate(flops=15 * 10**9, bytes_accessed=8 * 10**6, transcendentals=14 * 10**6),
    )(limit, *halos, *consts)


def swap(low, high, axis):
    count = lax.axis_size(axis)
    up = [(i, i + 1) for i in range(count - 1)]
    down = [(i + 1, i) for i in range(count - 1)]
    return lax.ppermute(high, axis, up), lax.ppermute(low, axis, down)


def on_device(latent, norm_gain, norm_shift, w_qkv, w_out, b_out, depth_limit):
    zlow, zhigh = swap(*z_faces(latent), "gz")
    own0, own1, held = arrange(latent)
    xlow, xhigh = swap(own0, own1, "gx")
    step = 1
    while step < lax.axis_size("gy"):
        pairs = [(i, i ^ step) for i in range(lax.axis_size("gy"))]
        held = jnp.concatenate([held, lax.ppermute(held, "gy", pairs)], axis=0)
        step *= 2
    rest = ("gx", "gz")
    rows = jax.ShapeDtypeStruct((lax.axis_size(rest), 128), f32)
    kernel = functools.partial(edges_kernel, float(latent.size // 32))
    *edges, rows = faces(kernel, (2, 4, 64, 256), (held, zlow, zhigh), rows)
    xzlow, xzhigh = swap(*edges, "gx")
    every = lax.all_to_all(rows, rest, 0, 0, tiled=True)
    near = (own0, own1, zlow, zhigh, xlow, xhigh, xzlow, xzhigh)
    ylow, yhigh = swap(*faces(y_faces_kernel, (4, 6, 64, 256), near), "gy")
    consts = (
        every,
        norm_gain[None],
        norm_shift[None],
        w_qkv,
        w_out,
        b_out[None],
    )
    ends = tuple(lax.axis_size(axis) - 1 for axis in AXES)
    middle = attend(ends, False, depth_limit, near, *consts)
    return attend(ends, True, depth_limit, near + (ylow, yhigh, middle), *consts)


def solution(mesh):
    placed = (P("gx", "gy", "gz", None), P(), P(), P(), P(), P(), P("gx", "gy", "gz"))
    return jax.shard_map(
        on_device, mesh=mesh, in_specs=placed, out_specs=P("gx", "gy", "gz", None), check_vma=False
    )
```

```python
import functools

import jax
import jax.numpy as jnp
import numpy as np
from jax import lax
from jax.experimental import pallas as pl
from jax.experimental.pallas import tpu as pltpu
from jax.sharding import PartitionSpec as P

GROUPS = 32
AXES = ("gx", "gy", "gz")
f32, bf = jnp.float32, jnp.bfloat16
NT = (((1,), (1,)), ((), ()))
SCALE = float(np.log2(np.e) / np.sqrt(32.0))
VMEM = pl.BlockSpec(memory_space=pltpu.VMEM)
SMEM = pl.BlockSpec(memory_space=pltpu.SMEM)
HBM = pl.BlockSpec(memory_space=pl.ANY)


def iota(shape, dim):
    return lax.broadcasted_iota(jnp.int32, shape, dim)


def exact_dot(a, b):
    return jnp.dot(a, b, precision=lax.Precision.HIGHEST, preferred_element_type=f32)


def low_rows(a, b):
    return jnp.where(iota(a.shape, 0) < 4, a, pltpu.roll(b, 4, 0))


def high_rows(a, b):
    return jnp.where(iota(a.shape, 0) < 4, pltpu.roll(a, 4, 0), b)


def block_rows(x_ref, x, y, half):
    lows, highs = [], []
    for pair in range(2):
        a, b = [x_ref[x, y + pair * 2 + k, half * 8 : half * 8 + 8].astype(f32) for k in range(2)]
        lows.append(low_rows(a, b))
        highs.append(high_rows(a, b))
    return [jnp.concatenate(parts, axis=0).astype(bf) for parts in (lows, highs)]


def z_faces_kernel(x_ref, low_ref, high_ref):
    for bx in range(2):
        for by in range(4):
            for x in range(4):
                rows = slice(x * 16, x * 16 + 16)
                low_ref[bx, by, rows] = block_rows(x_ref, bx * 4 + x, by * 4, 0)[0]
                high_ref[bx, by, rows] = block_rows(x_ref, bx * 4 + x, by * 4, 1)[1]


def z_faces(latent):
    face = jax.ShapeDtypeStruct((2, 4, 64, 256), bf)
    return pl.pallas_call(
        z_faces_kernel,
        out_shape=[face, face],
        in_specs=[VMEM],
        out_specs=[VMEM] * 2,
        compiler_params=pltpu.CompilerParams(vmem_limit_bytes=16 * 2**20),
    )(latent)


def arrange_kernel(x_ref, own0_ref, own1_ref, row_ref):
    for bx, own_ref in enumerate((own0_ref, own1_ref)):
        for by in range(4):
            for x in range(4):
                for half in range(2):
                    for k, piece in enumerate(block_rows(x_ref, bx * 4 + x, by * 4, half)):
                        own_ref[by, half * 2 + k, x * 16 : x * 16 + 16] = piece
    entries = 2048 * 8

    def sums(i, acc):
        return acc + jnp.sum(x_ref[i].astype(f32).reshape(32, 8, 256), axis=0)

    zeros = jnp.zeros((8, 256), f32)
    total = lax.fori_loop(0, 8, sums, zeros)
    total = jnp.broadcast_to(jnp.sum(total, axis=0, keepdims=True), (8, 256)) * (1.0 / entries)
    same = (iota((256, 256), 0) // 8 == iota((256, 256), 1) // 8).astype(f32)
    mean = exact_dot(total, same)

    def squares(i, acc):
        cells = x_ref[i].astype(f32) - mean[:1][None]
        return acc + jnp.sum((cells * cells).reshape(32, 8, 256), axis=0)

    acc = lax.fori_loop(0, 8, squares, zeros)
    acc = jnp.broadcast_to(jnp.sum(acc, axis=0, keepdims=True), (8, 256))
    first = (iota((256, 128), 0) // 8 == iota((256, 128), 1)).astype(f32)
    second = (iota((256, 128), 0) // 8 + 32 == iota((256, 128), 1)).astype(f32)
    row = exact_dot(total, first) + exact_dot(acc, second)
    row_ref[...] = jnp.broadcast_to(row[:1], row_ref.shape)


def arrange(latent):
    own = jax.ShapeDtypeStruct((4, 4, 64, 256), bf)
    return pl.pallas_call(
        arrange_kernel,
        out_shape=[own, own, jax.ShapeDtypeStruct((8, 128), f32)],
        in_specs=[VMEM],
        out_specs=[VMEM] * 3,
        compiler_params=pltpu.CompilerParams(vmem_limit_bytes=16 * 2**20),
    )(latent)


def edges_kernel(entries, held_ref, zlow, zhigh, low_ref, high_ref, rows_ref):
    for x, out in enumerate((low_ref, high_ref)):
        out[0], out[1] = zlow[x], zhigh[x]
    held = held_ref[...]
    share = 1.0 / held.shape[0]
    total = jnp.sum(held, axis=0, keepdims=True)
    apart = held - total * share
    spread = jnp.sum(apart * apart, axis=0, keepdims=True) * (entries / 8)
    total, spread = jnp.broadcast_to(total, (8, 128)), jnp.broadcast_to(spread, (8, 128))
    lane = iota((8, 128), 1)
    merged = jnp.where(lane < 64, total * (1.0 / 8) + pltpu.roll(spread, 32, 1), 0.0)
    merged = jnp.where(lane < 32, total * share, merged)
    rows_ref[...] = jnp.broadcast_to(merged[:1], rows_ref.shape)


def y_faces_kernel(own0, own1, zlow, zhigh, xlow, xhigh, xzlow, xzhigh, low_ref, high_ref):
    for y, out in ((0, low_ref), (3, high_ref)):
        for x, (inner, zhalo) in enumerate(((xlow, xzlow), (own0, None), (own1, None), (xhigh, xzhigh))):
            out[x, 1:5] = inner[y]
            out[x, 0] = zlow[x - 1, y] if zhalo is None else zhalo[0, y]
            out[x, 5] = zhigh[x - 1, y] if zhalo is None else zhalo[1, y]


def faces(kernel, shape, parts, *more):
    face = jax.ShapeDtypeStruct(shape, bf)
    return pl.pallas_call(
        kernel,
        out_shape=[face, face, *more],
        in_specs=[VMEM] * len(parts),
        out_specs=[VMEM] * (2 + len(more)),
        compiler_params=pltpu.CompilerParams(vmem_limit_bytes=16 * 2**20),
    )(*parts)


def interleave(*stages):
    stages = list(stages)
    while stages:
        for stage in list(stages):
            if next(stage, True):
                stages.remove(stage)


def attend_kernel(ends, edge, limit, *refs):
    halos, refs = (refs[:11], refs[11:]) if edge else (refs[:8], refs[8:])
    own0, own1, zlow, zhigh, xlow, xhigh, xzlow, xzhigh, *late = halos
    consts, (out_ref, *refs) = refs[:6], refs[6:]
    x_ref, k_ref, vt_ref, qbd_ref, om_ref, s_ref, p_ref, m_ref, lists, sems, wqT, wvT, *held = refs
    every, gain, shift_ref, w_qkv, wo, bo = held
    copies = list(zip(consts, held)) + [
        (own0, x_ref.at[1, 1:5, 1:5]),
        (own1, x_ref.at[2, 1:5, 1:5]),
        (zlow, x_ref.at[1:3, 1:5, 0]),
        (zhigh, x_ref.at[1:3, 1:5, 5]),
        (xlow, x_ref.at[0, 1:5, 1:5]),
        (xhigh, x_ref.at[3, 1:5, 1:5]),
        (xzlow.at[0], x_ref.at[0, 1:5, 0]),
        (xzlow.at[1], x_ref.at[0, 1:5, 5]),
        (xzhigh.at[0], x_ref.at[3, 1:5, 0]),
        (xzhigh.at[1], x_ref.at[3, 1:5, 5]),
    ]
    if edge:
        done = late.pop()
        copies += list(zip(late, (x_ref.at[:, 0], x_ref.at[:, 5])))
    copies = [pltpu.make_async_copy(a, b, sems.at[i]) for i, (a, b) in enumerate(copies)]
    for copy in copies:
        copy.start()

    spots = [lax.axis_index(axis) for axis in AXES]
    first = [(spot == 0).astype(jnp.int32) for spot in spots]
    last = [(spot == end).astype(jnp.int32) for spot, end in zip(spots, ends)]

    def place(dim, inner, i):
        out = jnp.where(i == 0, first[dim], jnp.where(i == inner + 1, last[dim], 0))
        return 1 - out, jnp.where(out == 0, i, jnp.where(i == 0, 1, inner))

    for copy in copies[:4]:
        copy.wait()
    wqT[...] = w_qkv[:, :256].astype(f32).T.astype(bf)
    wvT[...] = w_qkv[:, 512:].astype(f32).T.astype(bf)
    held_by = every.shape[0]
    entries = 2048.0 * 8.0 * (256 // held_by)
    rows = every[...]
    means = jnp.sum(rows, axis=0, keepdims=True) * (1.0 / held_by)
    apart = rows - means
    spread = jnp.sum(apart * apart, axis=0, keepdims=True)
    first_of = (iota((128, 256), 0) == iota((128, 256), 1) // 8).astype(f32)
    second_of = (iota((128, 256), 0) == iota((128, 256), 1) // 8 + 32).astype(f32)
    means8, spread8 = jnp.broadcast_to(means, (8, 128)), jnp.broadcast_to(spread, (8, 128))
    mean = exact_dot(means8, first_of)[:1]
    var = (exact_dot(means8, second_of)[:1] * (held_by / entries) + exact_dot(spread8, first_of)[:1]) * (1.0 / held_by)
    mul = lax.rsqrt(var + 1e-06) * gain[...]
    shift = shift_ref[...]

    bys = (0, 3) if edge else (1, 2)

    def sort(i, counts):
        deep, flat = counts
        bx, k, bz = i // 8, (i // 4) % 2, i % 4
        by = k * 3 if edge else k + 1
        spot = bx * 16 + by * 4 + bz
        lists[0, deep] = spot
        lists[1, flat] = spot
        is_deep = (limit[bx, by, bz] != 0).astype(jnp.int32)
        return deep + is_deep, flat + 1 - is_deep

    zero = jnp.int32(0)
    deep, flat = lax.fori_loop(0, 16, sort, (zero, zero))

    own_head = iota((256, 512), 0) // 32 == iota((256, 512), 1) // 64
    diag = iota((128, 256), 0) // 32 == iota((128, 256), 1) // 64
    for copy in copies[4:16]:
        copy.wait()

    def normed(cells):
        return ((cells.astype(f32) - mean) * mul + shift).astype(bf)

    lane = iota((1, 256), 1) // 64
    marks = jnp.zeros((1, 256), f32)
    for i in range(4):
        marks = jnp.where(lane == i, place(0, 2, i)[0].astype(f32), marks)
    tick = iota((16, 256), 0) == 0

    def prep_column(c, carry):
        y, z = c // 6, c % 6
        (y_in, y_from), (z_in, z_from) = place(1, 4, y), place(2, 4, z)
        n = normed(
            jnp.concatenate([x_ref[place(0, 2, i)[1], y_from, z_from] for i in range(4)], axis=0)
        )
        k_ref[c] = jnp.dot(n, w_qkv[:, 256:512], preferred_element_type=f32).astype(bf)
        valid = marks * (y_in * z_in).astype(f32)
        vt = lax.dot_general(wvT[...], n, NT, preferred_element_type=f32) * valid
        ones = jnp.where(tick, jnp.broadcast_to(valid, (16, 256)), 0.0)
        for g in range(2):
            t = jnp.concatenate([vt[g * 128 : (g + 1) * 128], ones], axis=0)
            vt_ref[0, c, g] = t[:, :192].astype(bf)
            vt_ref[1, c, g] = pltpu.roll(t, 192, 1)[:, :192].astype(bf)
        return carry

    lax.fori_loop(6, 30, prep_column, 0, unroll=24)

    def prep_query(i, carry):
        bx, k, bz = i // 8, (i // 4) % 2, i % 4
        by = k * 3 if edge else k + 1
        n = normed(x_ref[bx + 1, by + 1, bz + 1])
        q = lax.dot_general(wqT[...], jnp.concatenate([n] * 4, axis=0), NT, preferred_element_type=f32) * SCALE
        qbd_ref[bx * 16 + by * 4 + bz] = jnp.where(own_head, jnp.concatenate([q, q], axis=1), 0.0).astype(bf)
        return carry

    lax.fori_loop(0, 16, prep_query, 0, unroll=16)
    if edge:
        for copy in copies[16:]:
            copy.wait()
        lax.fori_loop(0, 12, lambda t, carry: prep_column(jnp.where(t < 6, t, t + 24), carry), 0, unroll=12)

    def columns(i, cols):
        by, bz = (i // 4) % 4, i % 4
        return [(by + dy) * 6 + bz + dz for dy, dz in cols]

    def scores(blocks, cols):
        for k, i in enumerate(blocks):
            rows = pl.ds(pl.multiple_of(i // 16 * 64, 64), 192)
            q, m, spots = qbd_ref[i], None, columns(i, cols)
            for j in range(0, len(cols), 3):
                keys = jnp.concatenate([k_ref[c, rows] for c in spots[j : j + 3]], axis=0)
                s = jnp.dot(keys, q, preferred_element_type=f32)
                s_ref[k * 576 + j * 192 : k * 576 + (j + 3) * 192] = s
                top = jnp.max(s.reshape(-1, 8, 512), axis=0)
                m = top if m is None else jnp.maximum(m, top)
                yield False
            m_ref[k] = jnp.broadcast_to(jnp.max(m, axis=0, keepdims=True), (8, 512))

    def weights(blocks, cols):
        for k in range(len(blocks)):
            top = m_ref[k][:1]
            for j in range(0, len(cols), 3):
                part = slice(k * 576 + j * 192, k * 576 + (j + 3) * 192)
                p_ref[part] = jnp.exp2(s_ref[part] - top).astype(bf)
                yield False

    def mix(blocks, cols):
        for k, i in enumerate(blocks):
            o = [None, None]
            for j, c in enumerate(columns(i, cols)):
                for g in range(2):
                    part = jnp.dot(
                        vt_ref[i // 16, c, g],
                        p_ref[k * 576 + j * 192 : k * 576 + (j + 1) * 192, g * 256 : (g + 1) * 256],
                        preferred_element_type=f32,
                    )
                    o[g] = part if o[g] is None else o[g] + part
                if j % 3 == 2:
                    yield False
            for g in range(2):
                om_ref[i, g] = jnp.where(diag, o[g][:128] * (1.0 / o[g][128:129]), 0.0).astype(bf)

    def run(which, count, cols, width):
        steps = (count + width - 1) // width

        def spots(t):
            return [lists[which, jnp.clip(t * width + k, 0, count - 1)] for k in range(width)]

        def step(t, carry):
            interleave(mix(spots(t - 2), cols), weights(spots(t - 1), cols), scores(spots(t), cols))
            return carry

        @pl.when(count > 0)
        def _():
            interleave(scores(spots(0), cols))
            interleave(weights(spots(0), cols), scores(spots(jnp.minimum(1, steps - 1)), cols))
            lax.fori_loop(2, steps, step, 0)
            interleave(mix(spots(jnp.maximum(steps - 2, 0)), cols), weights(spots(steps - 1), cols))
            interleave(mix(spots(steps - 1), cols))

    run(0, deep, [(dy, dz) for dz in range(3) for dy in range(3)], 1)
    run(1, flat, [(dy, 1) for dy in range(3)], 2)

    pick = jnp.where(iota((64, 256), 0) == iota((64, 256), 1) % 64, 1.0, 0.0).astype(bf)
    if edge:
        out_ref[:, 4:12] = done[...]

    def finish(i, carry):
        bx, k = i // 2, i % 2
        by = k * 3 if edge else k + 1
        spot = bx * 16 + by * 4
        mixed = [
            jnp.concatenate(
                [lax.dot_general(pick, om_ref[spot + bz, g], NT, preferred_element_type=f32).astype(bf) for g in range(2)],
                axis=1,
            )
            for bz in range(4)
        ]
        out = jnp.dot(jnp.concatenate(mixed, axis=0), wo[...], preferred_element_type=f32) + bo[...]
        y0 = by * 4 if edge else k * 4
        for x in range(4):
            for pair in range(2):
                parts = [out[b * 64 + x * 16 + pair * 8 : b * 64 + x * 16 + pair * 8 + 8] for b in range(4)]
                for which, join in enumerate((low_rows, high_rows)):
                    line = jnp.concatenate([join(parts[0], parts[1]), join(parts[2], parts[3])], axis=0)
                    out_ref[bx * 4 + x, y0 + pair * 2 + which] = line.astype(bf)
        return carry

    lax.fori_loop(0, 4, finish, 0, unroll=4)


def attend(ends, edge, limit, halos, *consts):
    out_y = 16 if edge else 8
    return pl.pallas_call(
        functools.partial(attend_kernel, ends, edge),
        out_shape=jax.ShapeDtypeStruct((8, out_y, 16, 256), bf),
        in_specs=[SMEM] + [VMEM if half.shape[0] == 8 else HBM for half in halos] + [HBM] * len(consts),
        out_specs=VMEM,
        scratch_shapes=[
            pltpu.VMEM((4, 6, 6, 64, 256), bf),
            pltpu.VMEM((36, 256, 256), bf),
            pltpu.VMEM((2, 36, 2, 144, 192), bf),
            pltpu.VMEM((32, 256, 512), bf),
            pltpu.VMEM((32, 2, 128, 256), bf),
            pltpu.VMEM((1728, 512), f32),
            pltpu.VMEM((1728, 512), bf),
            pltpu.VMEM((3, 8, 512), f32),
            pltpu.SMEM((2, 17), jnp.int32),
            pltpu.SemaphoreType.DMA((18,)),
            pltpu.VMEM((256, 256), bf),
            pltpu.VMEM((256, 256), bf),
        ]
        + [pltpu.VMEM(const.shape, const.dtype) for const in consts],
        compiler_params=pltpu.CompilerParams(vmem_limit_bytes=50 * 2**20),
        cost_estimate=pl.CostEstimate(flops=15 * 10**9, bytes_accessed=8 * 10**6, transcendentals=14 * 10**6),
    )(limit, *halos, *consts)


def swap(low, high, axis):
    count = lax.axis_size(axis)
    up = [(i, i + 1) for i in range(count - 1)]
    down = [(i + 1, i) for i in range(count - 1)]
    return lax.ppermute(high, axis, up), lax.ppermute(low, axis, down)


def on_device(latent, norm_gain, norm_shift, w_qkv, w_out, b_out, depth_limit):
    zlow, zhigh = swap(*z_faces(latent), "gz")
    own0, own1, held = arrange(latent)
    xlow, xhigh = swap(own0, own1, "gx")
    step = 1
    while step < lax.axis_size("gy"):
        pairs = [(i, i ^ step) for i in range(lax.axis_size("gy"))]
        held = jnp.concatenate([held, lax.ppermute(held, "gy", pairs)], axis=0)
        step *= 2
    rest = ("gx", "gz")
    rows = jax.ShapeDtypeStruct((lax.axis_size(rest), 128), f32)
    kernel = functools.partial(edges_kernel, float(latent.size // 32))
    *edges, rows = faces(kernel, (2, 4, 64, 256), (held, zlow, zhigh), rows)
    xzlow, xzhigh = swap(*edges, "gx")
    every = lax.all_to_all(rows, rest, 0, 0, tiled=True)
    near = (own0, own1, zlow, zhigh, xlow, xhigh, xzlow, xzhigh)
    ylow, yhigh = swap(*faces(y_faces_kernel, (4, 6, 64, 256), near), "gy")
    consts = (
        every,
        norm_gain[None],
        norm_shift[None],
        w_qkv,
        w_out,
        b_out[None],
    )
    ends = tuple(lax.axis_size(axis) - 1 for axis in AXES)
    middle = attend(ends, False, depth_limit, near, *consts)
    return attend(ends, True, depth_limit, near + (ylow, yhigh, middle), *consts)


def solution(mesh):
    placed = (P("gx", "gy", "gz", None), P(), P(), P(), P(), P(), P("gx", "gy", "gz"))
    return jax.shard_map(
        on_device, mesh=mesh, in_specs=placed, out_specs=P("gx", "gy", "gz", None), check_vma=False
    )
```
